32 devices in a mesh: clip: 2 (over x), seq: 16 (over z, y, core).
Axes of the slice: x: 2, y: 2, z: 4, core: 2. Of those that a mesh axis runs over, the one named last changes fastest.
Arguments:
- spatial_saved: bfloat16 [3, 32, 256, 576], P(None, ('clip', 'seq')), parts along dimension 1, may hold values from -48 to 48
- hidden: bfloat16 [32, 256, 1152], P(('clip', 'seq')), parts along dimension 0, may hold values from -6 to 6
- temporal_out_grad: bfloat16 [32, 256, 576], P(('clip', 'seq')), parts along dimension 0, may hold values from -6 to 6
- stream_grad: bfloat16 [32, 256, 1152], P(('clip', 'seq')), parts along dimension 0, may hold values from -6 to 6
- modulation: float32 [1152], replicated, may hold values from -0.5 to 1
- temporal_weights: bfloat16 [1152, 1728], P('seq'), may hold values from -0.1875 to 0.1875
- spatial_weights: bfloat16 [576, 1152], P('seq'), may hold values from -0.25 to 0.25
Outputs:
- hidden_grad: bfloat16 [32, 256, 1152], P(('clip', 'seq')), parts along dimension 0
- spatial_grad: bfloat16 [3, 32, 256, 576], P(None, ('clip', 'seq')), parts along dimension 1
The draws below stay inside these ranges and needn't reach their ends.
There are 2 independent parts, one for each index of `clip`. The reference program is written for one: setup_inputs(seed, part) draws one part's arguments, and reference() takes and returns one part's arrays. A program takes and returns all parts, laid end to end along the dimension named above; an argument that names none is the same for every part. Nothing has to cross between parts.
All inputs are finite; a program needn't handle non-finite values.
Results may differ from the reference program's by a relative error of at most 0.024.
Values may be sent and summed in bfloat16 or wider, within the bound.
No kernel may reach another device: no remote copies, remote signals or barrier semaphores. Data moves between devices by JAX's collectives and lax.ppermute only.
A program may use at most 64 MiB of HBM per device.

```python
import math
import jax
import jax.numpy as jnp
from jax import lax

D = 1152
HEADS = 8
HD = 72
PATCH = 256
FRAMES = 16
AW = 576


def draw_spatial_saved(key, part):
    shape = (3, FRAMES, PATCH, HEADS * HD)
    return jnp.clip(jax.random.normal(key, shape, jnp.float32), -4.0, 4.0).astype(jnp.bfloat16)


def draw_modulation(key, part):
    return jax.random.uniform(key, (D,), jnp.float32, -0.5, 0.5)


def level_of(stream_key, dims, cuts, low, top_value):
    factor_of, own = 1.0, jax.random.fold_in(stream_key, 6)
    for dim, parts in cuts:
        heights = jnp.exp(jax.random.uniform(jax.random.fold_in(own, dim), (parts,), jnp.float32, low / len(cuts), top_value / len(cuts)))
        factor_of = factor_of * jnp.repeat(heights, dims[dim] // parts).reshape([-1 if axis == dim else 1 for axis in range(len(dims))])
    return factor_of


def normal_values(own_key, dims, scale, most, shards=(), dtype=jnp.bfloat16):
    values = scale * jax.random.normal(own_key, dims, jnp.float32)
    if shards:
        values = values * level_of(own_key, dims, shards, -0.22, 0.18)
    return jnp.clip(values, -most, most).astype(dtype)


def setup_inputs(seed: int = 0, part: int = 0) -> dict:
    key_of = jax.random.split(jax.random.key(seed), 8)
    part_keys = jax.random.split(jax.random.fold_in(key_of[7], part), 8)
    spatial_saved = draw_spatial_saved(jax.random.fold_in(jax.random.fold_in(key_of[7], part), 71), part)
    hidden = normal_values(part_keys[1], (FRAMES, PATCH, D), 1.0, 6.0, ((0, 16),))
    temporal_out_grad = normal_values(part_keys[2], (FRAMES, PATCH, AW), 1.0, 6.0, ((0, 16),))
    stream_grad = normal_values(part_keys[3], (FRAMES, PATCH, D), 1.0, 6.0, ((0, 16),))
    modulation = draw_modulation(jax.random.fold_in(key_of[7], 71), part)
    temporal_weights = normal_values(key_of[5], (D, 3 * AW), D ** -0.5, 0.1875, ((0, 16),))
    spatial_weights = normal_values(key_of[6], (AW, D), AW ** -0.5, 0.25, ((0, 16),))
    return dict(spatial_saved=spatial_saved, hidden=hidden, temporal_out_grad=temporal_out_grad, stream_grad=stream_grad, modulation=modulation, temporal_weights=temporal_weights, spatial_weights=spatial_weights)


epsilon = 1e-06

def attend_grad(query, keys, values, grad_o, form):
    query = query.astype(jnp.float32)
    keys = keys.astype(jnp.float32)
    values = values.astype(jnp.float32)
    grad_o = grad_o.astype(jnp.float32)
    key_form = form.replace('l', 'm')
    scale = 1.0 / math.sqrt(query.shape[-1])
    scores = jnp.einsum(form + ',' + key_form + '->bhlm', query, keys) * scale
    attention = jax.nn.softmax(scores, axis=-1)
    rounded = attention.astype(jnp.bfloat16).astype(jnp.float32)
    output = jnp.einsum('bhlm,' + key_form + '->' + form, rounded, values)
    delta = jnp.einsum(form + ',' + form + '->bhl', grad_o, output)
    spread = jnp.einsum(form + ',' + key_form + '->bhlm', grad_o, values)
    dscore = (attention * (spread - delta[..., None])).astype(jnp.bfloat16).astype(jnp.float32)
    grad_query = (jnp.einsum('bhlm,' + key_form + '->' + form, dscore, keys) * scale).astype(jnp.bfloat16)
    grad_keys = (jnp.einsum('bhlm,' + form + '->' + key_form, dscore, query) * scale).astype(jnp.bfloat16)
    grad_values = jnp.einsum('bhlm,' + form + '->' + key_form, rounded, grad_o).astype(jnp.bfloat16)
    return (grad_query, grad_keys, grad_values)

def split_heads(block):
    return block.reshape(block.shape[:-1] + (HEADS, HD))

def merge_heads(block):
    return block.reshape(block.shape[:-2] + (HEADS * HD,))

def layer_norm(hidden, modulation):
    widened = hidden.astype(jnp.float32)
    mean_value = lax.optimization_barrier(jnp.mean(widened, axis=-1, keepdims=True))
    centered = widened - mean_value
    inverse = lax.rsqrt(lax.optimization_barrier(jnp.mean(centered * centered, axis=-1, keepdims=True)) + epsilon)
    normal_form = centered * inverse
    normed = (normal_form * (1.0 + modulation.astype(jnp.float32))).astype(jnp.bfloat16)
    return (normed, normal_form, inverse)

def norm_back(grad_normed, normal_form, inverse, modulation):
    scaled = grad_normed * (1.0 + modulation.astype(jnp.float32))
    return inverse * (scaled - lax.optimization_barrier(jnp.mean(scaled, axis=-1, keepdims=True)) - normal_form * lax.optimization_barrier(jnp.mean(scaled * normal_form, axis=-1, keepdims=True)))

def reference(spatial_saved, hidden, temporal_out_grad, stream_grad, modulation, temporal_weights, spatial_weights):
    width = HEADS * HD
    normed, normal_form, inverse = layer_norm(hidden, modulation)
    projected = jnp.dot(normed.reshape(-1, D), temporal_weights, preferred_element_type=jnp.float32)
    projected = projected.astype(jnp.bfloat16).reshape(FRAMES, PATCH, 3 * width)
    grads = attend_grad(split_heads(projected[..., :width]), split_heads(projected[..., width:2 * width]), split_heads(projected[..., 2 * width:]), split_heads(temporal_out_grad), 'lbhd')
    projection_grads = jnp.concatenate([merge_heads(gradient) for gradient in grads], axis=-1)
    norm_grad = jnp.dot(projection_grads.reshape(-1, 3 * width), temporal_weights.T, preferred_element_type=jnp.float32).reshape(FRAMES, PATCH, D)
    branch = norm_back(norm_grad, normal_form, inverse, modulation).astype(jnp.bfloat16)
    branch = lax.optimization_barrier(branch)
    hidden_grad = (stream_grad.astype(jnp.float32) + branch.astype(jnp.float32)).astype(jnp.bfloat16)
    attention_grad = jnp.dot(hidden_grad.reshape(-1, D), spatial_weights.T, preferred_element_type=jnp.float32)
    attention_grad = attention_grad.astype(jnp.bfloat16).reshape(FRAMES, PATCH, width)
    spatial = attend_grad(split_heads(spatial_saved[0]), split_heads(spatial_saved[1]), split_heads(spatial_saved[2]), split_heads(attention_grad), 'blhd')
    spatial_grad = jnp.stack([merge_heads(gradient) for gradient in spatial])
    return (hidden_grad, spatial_grad)
```

```python
import functools
import math

import jax
import jax.numpy as jnp
from jax import lax
from jax.experimental import pallas as pl
from jax.experimental.pallas import tpu as pltpu
from jax.sharding import PartitionSpec as P

HEADS = 8
HD = 72
LANES = 128

epsilon = 1e-06
VMEM_LIMIT = 48 * 1024 * 1024


def window(head, width):
    low, high = head * HD, (head + 1) * HD
    start = low // LANES * LANES
    stop = min(-(-high // LANES) * LANES, width)
    return start, stop, low, high


def keep(block, start, low, high):
    lane = lax.broadcasted_iota(jnp.int32, block.shape, 1) + start
    return jnp.where((lane >= low) & (lane < high), block, jnp.zeros_like(block))


def dot_nt(a, b):
    return lax.dot_general(a, b, (((1,), (1,)), ((), ())), preferred_element_type=jnp.float32)


def dot_tn(a, b):
    return lax.dot_general(a, b, (((0,), (0,)), ((), ())), preferred_element_type=jnp.float32)


def dot_nn(a, b):
    return jnp.dot(a, b, preferred_element_type=jnp.float32)


def soft(scores_t, scale):
    top = jnp.max(scores_t, axis=0, keepdims=True)
    raised = jnp.exp2((scores_t - top) * (scale * math.log2(math.e)))
    return raised * (1.0 / jnp.sum(raised, axis=0, keepdims=True))


class Tiles:
    def __init__(self):
        self.sums = {}

    def add(self, start, part):
        for offset in range(0, part.shape[1], LANES):
            piece = part[:, offset : offset + LANES]
            key = start + offset
            self.sums[key] = self.sums[key] + piece if key in self.sums else piece

    def store(self, ref, base, width, scale, upto):
        for key in sorted(self.sums):
            stop = min(key + LANES, width)
            if stop <= upto:
                done = self.sums.pop(key)[:, : stop - key] * scale
                ref[:, base + key : base + stop] = done.astype(ref.dtype)


def head_grads(attention_t, query, keys, values, grad_o, start, low, high):
    rounded_t = attention_t.astype(jnp.bfloat16)
    spread_t = dot_nt(keep(values, start, low, high), grad_o)
    wide = rounded_t.astype(jnp.float32)
    delta = jnp.sum(wide * spread_t, axis=0, keepdims=True)
    dscore_t = (attention_t.astype(jnp.float32) * (spread_t - delta)).astype(jnp.bfloat16)
    return (
        dot_tn(dscore_t, keep(keys, start, low, high)),
        dot_nn(dscore_t, keep(query, start, low, high)),
        dot_nn(rounded_t, keep(grad_o, start, low, high)),
    )


def temporal_kernel(patches, x_ref, mod_ref, w_ref, out_ref, bias_ref, proj_ref, keys_ref, grad_ref, gk_ref):
    tokens, width = out_ref.shape[0], w_ref.shape[1] // 3
    depth = w_ref.shape[0]
    scale = 1.0 / math.sqrt(HD)
    row = lax.broadcasted_iota(jnp.int32, (tokens, tokens), 0)
    column = lax.broadcasted_iota(jnp.int32, (tokens, tokens), 1)
    bias_ref[...] = jnp.where(lax.rem(row, patches) == lax.rem(column, patches), 0.0, -1e30)
    gain = 1.0 + mod_ref[...]
    widened = x_ref[:, :depth].astype(jnp.float32)
    centered = widened - jnp.mean(widened, axis=-1, keepdims=True)
    inverse = lax.rsqrt(jnp.mean(centered * centered, axis=-1, keepdims=True) + epsilon)
    normed = (centered * inverse * gain).astype(jnp.bfloat16)
    proj_ref[...] = dot_nn(normed, w_ref[...]).astype(jnp.bfloat16)
    keys_ref[...] = proj_ref[:, width : 2 * width]
    sums = [Tiles(), Tiles(), Tiles()]
    for head in range(HEADS):
        start, stop, low, high = window(head, width)
        query = proj_ref[:, start:stop]
        keys = keys_ref[:, start:stop]
        values = proj_ref[:, 2 * width + start : 2 * width + stop]
        grad_o = x_ref[:, depth + start : depth + stop]
        scores_t = dot_nt(keep(keys, start, low, high), query) + bias_ref[...]
        parts = head_grads(soft(scores_t, scale), query, keys, values, grad_o, start, low, high)
        for tiles, part in zip(sums, parts):
            tiles.add(start, part)
        upto = width if head == HEADS - 1 else high // LANES * LANES
        sums[0].store(grad_ref, 0, width, scale, upto)
        sums[1].store(gk_ref, 0, width, scale, upto)
        sums[2].store(grad_ref, 2 * width, width, 1.0, upto)
    grad_ref[:, width : 2 * width] = gk_ref[...]
    scaled = dot_nt(grad_ref[...], w_ref[...]) * gain
    widened = x_ref[:, :depth].astype(jnp.float32)
    centered = widened - jnp.mean(widened, axis=-1, keepdims=True)
    normal_form = centered * inverse
    branch = inverse * (
        scaled
        - jnp.mean(scaled, axis=-1, keepdims=True)
        - normal_form * jnp.mean(scaled * normal_form, axis=-1, keepdims=True)
    )
    out_ref[...] = branch.astype(out_ref.dtype)


def temporal(mixed, modulation, weights, patches):
    tokens, depth, width = mixed.shape[0], weights.shape[0], weights.shape[1] // 3
    return pl.pallas_call(
        functools.partial(temporal_kernel, patches),
        out_shape=jax.ShapeDtypeStruct((tokens, depth), jnp.bfloat16),
        scratch_shapes=[
            pltpu.VMEM((tokens, tokens), jnp.float32),
            pltpu.VMEM((tokens, 3 * width), jnp.bfloat16),
            pltpu.VMEM((tokens, width), jnp.bfloat16),
            pltpu.VMEM((tokens, 3 * width), jnp.bfloat16),
            pltpu.VMEM((tokens, width), jnp.bfloat16),
        ],
        compiler_params=pltpu.CompilerParams(vmem_limit_bytes=VMEM_LIMIT),
        cost_estimate=pl.CostEstimate(
            flops=12 * tokens * depth * width + 12 * HEADS * tokens * tokens * 2 * LANES,
            bytes_accessed=2 * (2 * tokens * 3 * width + 3 * depth * width),
            transcendentals=HEADS * tokens * tokens,
        ),
        name="temporal_backward",
    )(mixed, modulation.reshape(1, depth), weights)


def score_kernel(saved_ref, out_ref):
    width = saved_ref.shape[2]
    for head in range(HEADS):
        start, stop, low, high = window(head, width)
        keys = keep(saved_ref[1, :, start:stop], start, low, high)
        scores_t = dot_nt(keys, saved_ref[0, :, start:stop])
        out_ref[head] = soft(scores_t, 1.0 / math.sqrt(HD)).astype(out_ref.dtype)


def score(saved):
    tokens, width = saved.shape[1:]
    return pl.pallas_call(
        score_kernel,
        out_shape=jax.ShapeDtypeStruct((HEADS, tokens, tokens), jnp.bfloat16),
        compiler_params=pltpu.CompilerParams(vmem_limit_bytes=VMEM_LIMIT),
        cost_estimate=pl.CostEstimate(
            flops=2 * HEADS * tokens * tokens * 2 * LANES,
            bytes_accessed=2 * (3 * tokens * width + HEADS * tokens * tokens),
            transcendentals=HEADS * tokens * tokens,
        ),
        name="spatial_scores",
    )(saved)


def spatial_kernel(attention_ref, saved_ref, stream_ref, branch_ref, w_ref, hidden_ref, out_ref, grad_ref):
    width = saved_ref.shape[2]
    scale = 1.0 / math.sqrt(HD)
    hidden_grad = (
        stream_ref[...].astype(jnp.float32) + branch_ref[...].astype(jnp.float32)
    ).astype(jnp.bfloat16)
    hidden_ref[...] = hidden_grad
    grad_ref[...] = dot_nt(hidden_grad, w_ref[...]).astype(jnp.bfloat16)
    sums = [Tiles(), Tiles(), Tiles()]
    for head in range(HEADS):
        start, stop, low, high = window(head, width)
        parts = head_grads(
            attention_ref[head],
            saved_ref[0, :, start:stop],
            saved_ref[1, :, start:stop],
            saved_ref[2, :, start:stop],
            grad_ref[:, start:stop],
            start,
            low,
            high,
        )
        upto = width if head == HEADS - 1 else high // LANES * LANES
        for index, (tiles, part) in enumerate(zip(sums, parts)):
            tiles.add(start, part)
            tiles.store(out_ref.at[index], 0, width, 1.0 if index == 2 else scale, upto)


def spatial(attention_t, saved, stream, branch, weights):
    tokens, depth = stream.shape
    width = weights.shape[0]
    return pl.pallas_call(
        spatial_kernel,
        out_shape=(
            jax.ShapeDtypeStruct((tokens, depth), jnp.bfloat16),
            jax.ShapeDtypeStruct((3, tokens, width), jnp.bfloat16),
        ),
        scratch_shapes=[pltpu.VMEM((tokens, width), jnp.bfloat16)],
        compiler_params=pltpu.CompilerParams(vmem_limit_bytes=VMEM_LIMIT),
        cost_estimate=pl.CostEstimate(
            flops=2 * tokens * depth * width + 10 * HEADS * tokens * tokens * 2 * LANES,
            bytes_accessed=2 * (3 * tokens * depth + depth * width + 6 * tokens * width),
            transcendentals=0,
        ),
        name="spatial_backward",
    )(attention_t, saved, stream, branch, weights)


def shards(
    spatial_saved,
    hidden,
    temporal_out_grad,
    stream_grad,
    modulation,
    temporal_weights,
    spatial_weights,
):
    frames = lax.axis_size("seq")
    tokens, depth = hidden.shape[1:]
    width = temporal_out_grad.shape[2]
    patches = tokens // frames
    saved = spatial_saved.reshape(3, tokens, width)
    mixed = jnp.concatenate([hidden, temporal_out_grad], axis=2).reshape(frames, patches, depth + width)
    mixed = lax.all_to_all(mixed, "seq", split_axis=0, concat_axis=0, tiled=True)
    weights = lax.all_gather(temporal_weights, "seq", axis=0, tiled=True)
    attention_t = score(saved)
    branch = temporal(mixed.reshape(tokens, depth + width), modulation, weights, patches)
    branch = lax.all_to_all(
        branch.reshape(frames, patches, depth), "seq", split_axis=0, concat_axis=0, tiled=True
    )
    hidden_grad, spatial_grad = spatial(
        attention_t,
        saved,
        stream_grad.reshape(tokens, depth),
        branch.reshape(tokens, depth),
        lax.all_gather(spatial_weights, "seq", axis=0, tiled=True),
    )
    return (hidden_grad.reshape(1, tokens, depth), spatial_grad.reshape(3, 1, tokens, width))


def solution(mesh):
    return jax.shard_map(
        shards,
        mesh=mesh,
        in_specs=(
            P(None, ("clip", "seq"), None, None),
            P(("clip", "seq"), None, None),
            P(("clip", "seq"), None, None),
            P(("clip", "seq"), None, None),
            P(),
            P("seq", None),
            P("seq", None),
        ),
        out_specs=(P(("clip", "seq"), None, None), P(None, ("clip", "seq"), None, None)),
        check_vma=False,
    )
```

```python
import functools
import math

import jax
import jax.numpy as jnp
from jax import lax
from jax.experimental import pallas as pl
from jax.experimental.pallas import tpu as pltpu
from jax.sharding import PartitionSpec as P

HEADS = 8
HD = 72
LANES = 128

epsilon = 1e-06
VMEM_LIMIT = 32 * 1024 * 1024


def window(head, width):
    low, high = head * HD, (head + 1) * HD
    start = low // LANES * LANES
    stop = min(-(-high // LANES) * LANES, width)
    return start, stop, low, high


def keep(block, start, low, high):
    lane = lax.broadcasted_iota(jnp.int32, block.shape, 1) + start
    return jnp.where((lane >= low) & (lane < high), block, jnp.zeros_like(block))


def dot_nt(a, b):
    return lax.dot_general(a, b, (((1,), (1,)), ((), ())), preferred_element_type=jnp.float32)


def dot_tn(a, b):
    return lax.dot_general(a, b, (((0,), (0,)), ((), ())), preferred_element_type=jnp.float32)


def dot_nn(a, b):
    return jnp.dot(a, b, preferred_element_type=jnp.float32)


def soft(scores_t, scale):
    top = jnp.max(scores_t, axis=0, keepdims=True)
    raised = jnp.exp2((scores_t - top) * (scale * math.log2(math.e)))
    return raised * (1.0 / jnp.sum(raised, axis=0, keepdims=True))


class Tiles:
    def __init__(self):
        self.sums = {}

    def add(self, start, part):
        for offset in range(0, part.shape[1], LANES):
            piece = part[:, offset : offset + LANES]
            key = start + offset
            self.sums[key] = self.sums[key] + piece if key in self.sums else piece

    def store(self, ref, base, width, scale, upto):
        for key in sorted(self.sums):
            stop = min(key + LANES, width)
            if stop <= upto:
                done = self.sums.pop(key)[:, : stop - key] * scale
                ref[:, base + key : base + stop] = done.astype(ref.dtype)


def head_grads(attention_t, query, keys, values, grad_o, start, low, high):
    rounded_t = attention_t.astype(jnp.bfloat16)
    spread_t = dot_nt(keep(values, start, low, high), grad_o)
    wide = rounded_t.astype(jnp.float32)
    delta = jnp.sum(wide * spread_t, axis=0, keepdims=True)
    dscore_t = (attention_t.astype(jnp.float32) * (spread_t - delta)).astype(jnp.bfloat16)
    return (
        dot_tn(dscore_t, keep(keys, start, low, high)),
        dot_nn(dscore_t, keep(query, start, low, high)),
        dot_nn(rounded_t, keep(grad_o, start, low, high)),
    )


def temporal_kernel(patches, count, place_ref, x_ref, gain_ref, *refs):
    pieces, refs = refs[:count], refs[count:]
    out_ref, bias_ref, proj_ref, keys_ref, grad_ref, gk_ref, held_ref, sems = refs
    tokens, depth = out_ref.shape
    width = keys_ref.shape[1]
    scale = 1.0 / math.sqrt(HD)
    copies = []
    for index, piece in enumerate(pieces):
        for slot in range(piece.shape[0]):
            rows, columns = piece.shape[1:]
            number = len(copies)
            if rows == depth:
                copies.append(pltpu.make_async_copy(piece.at[slot], held_ref, sems.at[number]))
                copies[-1].start()
                continue
            row = pl.multiple_of(place_ref[2 * number], rows)
            column = pl.multiple_of(place_ref[2 * number + 1], columns)
            copies.append(
                pltpu.make_async_copy(
                    piece.at[slot],
                    held_ref.at[pl.ds(row, rows), pl.ds(column, columns)],
                    sems.at[number],
                )
            )
            copies[-1].start()
    row = lax.broadcasted_iota(jnp.int32, (tokens, tokens), 0)
    column = lax.broadcasted_iota(jnp.int32, (tokens, tokens), 1)
    bias_ref[...] = jnp.where(lax.rem(row, patches) == lax.rem(column, patches), 0.0, -1e30)
    gain = gain_ref[...]
    widened = x_ref[:, :depth].astype(jnp.float32)
    centered = widened - jnp.mean(widened, axis=-1, keepdims=True)
    inverse = lax.rsqrt(jnp.mean(centered * centered, axis=-1, keepdims=True) + epsilon)
    normed = (centered * inverse * gain).astype(jnp.bfloat16)
    for copy in copies:
        copy.wait()
    proj_ref[...] = dot_nn(normed, held_ref[:, : 3 * width]).astype(jnp.bfloat16)
    keys_ref[...] = proj_ref[:, width : 2 * width]
    sums = [Tiles(), Tiles(), Tiles()]
    for head in range(HEADS):
        start, stop, low, high = window(head, width)
        query = proj_ref[:, start:stop]
        keys = keys_ref[:, start:stop]
        values = proj_ref[:, 2 * width + start : 2 * width + stop]
        grad_o = x_ref[:, depth + start : depth + stop]
        scores_t = dot_nt(keep(keys, start, low, high), query) + bias_ref[...]
        parts = head_grads(soft(scores_t, scale), query, keys, values, grad_o, start, low, high)
        for tiles, part in zip(sums, parts):
            tiles.add(start, part)
        upto = width if head == HEADS - 1 else high // LANES * LANES
        sums[0].store(grad_ref, 0, width, scale, upto)
        sums[1].store(gk_ref, 0, width, scale, upto)
        sums[2].store(grad_ref, 2 * width, width, 1.0, upto)
    grad_ref[:, width : 2 * width] = gk_ref[...]
    scaled = dot_nt(grad_ref[...], held_ref[:, : 3 * width]) * gain
    widened = x_ref[:, :depth].astype(jnp.float32)
    centered = widened - jnp.mean(widened, axis=-1, keepdims=True)
    normal_form = centered * inverse
    branch = inverse * (
        scaled
        - jnp.mean(scaled, axis=-1, keepdims=True)
        - normal_form * jnp.mean(scaled * normal_form, axis=-1, keepdims=True)
    )
    out_ref[...] = branch.astype(out_ref.dtype)


def temporal(mixed, gain, pieces, places, width, patches):
    tokens, depth = mixed.shape[0], gain.shape[1]
    held = max(2 * pieces[0].shape[2], 3 * width) if len(pieces) > 1 else pieces[0].shape[2]
    count = sum(piece.shape[0] for piece in pieces)
    return pl.pallas_call(
        functools.partial(temporal_kernel, patches, len(pieces)),
        out_shape=jax.ShapeDtypeStruct((tokens, depth), jnp.bfloat16),
        in_specs=[pl.BlockSpec(memory_space=pltpu.SMEM)]
        + [pl.BlockSpec(memory_space=pltpu.VMEM)] * 2
        + [pl.BlockSpec(memory_space=pl.ANY)] * len(pieces),
        out_specs=pl.BlockSpec(memory_space=pltpu.VMEM),
        scratch_shapes=[
            pltpu.VMEM((tokens, tokens), jnp.float32),
            pltpu.VMEM((tokens, 3 * width), jnp.bfloat16),
            pltpu.VMEM((tokens, width), jnp.bfloat16),
            pltpu.VMEM((tokens, 3 * width), jnp.bfloat16),
            pltpu.VMEM((tokens, width), jnp.bfloat16),
            pltpu.VMEM((depth, held), jnp.bfloat16),
            pltpu.SemaphoreType.DMA((count,)),
        ],
        compiler_params=pltpu.CompilerParams(vmem_limit_bytes=VMEM_LIMIT),
        cost_estimate=pl.CostEstimate(
            flops=12 * tokens * depth * width + 12 * HEADS * tokens * tokens * 2 * LANES,
            bytes_accessed=2 * (2 * tokens * 3 * width + 3 * depth * width),
            transcendentals=HEADS * tokens * tokens,
        ),
        name="temporal_backward",
    )(places, mixed, gain, *pieces)


def prepare_kernel(count, place_ref, saved_ref, stream_ref, *refs):
    pieces, refs = refs[:count], refs[count:]
    attention_ref, values_ref, held_stream_ref, weights_ref, held_ref, sems = refs
    copies = []
    for piece in pieces:
        for slot in range(piece.shape[0]):
            number = len(copies)
            if piece.shape[2] == held_ref.shape[2]:
                target = held_ref.at[slot]
            else:
                column = pl.multiple_of(place_ref[2 * number + 1], piece.shape[2])
                target = held_ref.at[place_ref[2 * number], :, pl.ds(column, piece.shape[2])]
            copies.append(pltpu.make_async_copy(piece.at[slot], target, sems.at[number]))
            copies[-1].start()
    held_stream_ref[...] = stream_ref[...]
    for head in range(HEADS):
        scores_t = dot_tn(saved_ref[1, head], saved_ref[0, head])
        attention_ref[head] = soft(scores_t, 1.0 / math.sqrt(HD)).astype(attention_ref.dtype)
        values_ref[head] = saved_ref[2, head].astype(jnp.float32).T.astype(values_ref.dtype)
    for copy in copies:
        copy.wait()
    blocks = [held_ref[chip].astype(jnp.float32) for chip in range(held_ref.shape[0])]
    joined = jnp.concatenate(blocks, axis=0)[:, : weights_ref.shape[1]]
    weights_ref[...] = joined.astype(weights_ref.dtype)


def prepare(saved, stream, pieces, places, width):
    tokens, depth = stream.shape
    rows = pieces[0].shape[1]
    held = max(depth, pieces[0].shape[2] * (1 if len(pieces) == 1 else 2))
    count = sum(piece.shape[0] for piece in pieces)
    return pl.pallas_call(
        functools.partial(prepare_kernel, len(pieces)),
        out_shape=(
            jax.ShapeDtypeStruct((HEADS, tokens, tokens), jnp.bfloat16),
            jax.ShapeDtypeStruct((HEADS, tokens, HD), jnp.bfloat16),
            jax.ShapeDtypeStruct((tokens, depth), jnp.bfloat16),
            jax.ShapeDtypeStruct((width, depth), jnp.bfloat16),
        ),
        in_specs=[pl.BlockSpec(memory_space=pltpu.SMEM)]
        + [pl.BlockSpec(memory_space=pltpu.VMEM)] * 2
        + [pl.BlockSpec(memory_space=pl.ANY)] * len(pieces),
        out_specs=(pl.BlockSpec(memory_space=pltpu.VMEM),) * 4,
        scratch_shapes=[
            pltpu.VMEM((width // rows, rows, held), jnp.bfloat16),
            pltpu.SemaphoreType.DMA((count,)),
        ],
        compiler_params=pltpu.CompilerParams(vmem_limit_bytes=VMEM_LIMIT),
        cost_estimate=pl.CostEstimate(
            flops=2 * HEADS * tokens * tokens * 2 * LANES,
            bytes_accessed=2 * (4 * HEADS * tokens * HD + HEADS * tokens * tokens),
            transcendentals=HEADS * tokens * tokens,
        ),
        name="spatial_prepare",
    )(places, saved, stream, *pieces)


def spatial_kernel(attention_ref, values_ref, saved_ref, stream_ref, branch_ref, w_ref, hidden_ref, out_ref):
    scale = 1.0 / math.sqrt(HD)
    hidden_grad = (
        stream_ref[...].astype(jnp.float32) + branch_ref[...].astype(jnp.float32)
    ).astype(jnp.bfloat16)
    hidden_ref[...] = hidden_grad
    grad_all = dot_nt(w_ref[...], hidden_grad)
    for head in range(HEADS):
        grad_o = grad_all[head * HD : (head + 1) * HD].astype(jnp.bfloat16)
        rounded_t = attention_ref[head]
        wide = rounded_t.astype(jnp.float32)
        spread_t = dot_nn(values_ref[head], grad_o)
        delta = jnp.sum(wide * spread_t, axis=0, keepdims=True)
        dscore_t = (wide * (spread_t - delta)).astype(jnp.bfloat16)
        out_ref[0, head] = (dot_nn(saved_ref[1, head], dscore_t) * scale).astype(out_ref.dtype)
        out_ref[1, head] = (dot_nt(saved_ref[0, head], dscore_t) * scale).astype(out_ref.dtype)
        out_ref[2, head] = dot_nt(grad_o, rounded_t).astype(out_ref.dtype)


def spatial(attention_t, values, saved, stream, branch, weights):
    tokens, depth = stream.shape
    width = weights.shape[0]
    return pl.pallas_call(
        spatial_kernel,
        out_shape=(
            jax.ShapeDtypeStruct((tokens, depth), jnp.bfloat16),
            jax.ShapeDtypeStruct((3, HEADS, HD, tokens), jnp.bfloat16),
        ),
        compiler_params=pltpu.CompilerParams(vmem_limit_bytes=VMEM_LIMIT),
        cost_estimate=pl.CostEstimate(
            flops=2 * tokens * depth * width + 10 * HEADS * tokens * tokens * 2 * LANES,
            bytes_accessed=2 * (3 * tokens * depth + depth * width + 6 * tokens * width),
            transcendentals=0,
        ),
        name="spatial_backward",
    )(attention_t, values, saved, stream, branch, weights)


def moved(block, clips, devices, target):
    pairs = []
    for clip in range(clips):
        for own in range(devices):
            x, y, z, core = target(clip, own // 2 % 2, own // 4, own % 2)
            pairs.append((clip * devices + own, x * devices + (2 * z + y) * 2 + core))
    return lax.ppermute(block, ("clip", "seq"), pairs)


class Gather:
    def __init__(self, clips, devices):
        self.send = functools.partial(moved, clips=clips, devices=devices)
        clip, own = lax.axis_index("clip"), lax.axis_index("seq")
        self.x, self.core, self.y, self.z = clip % 2, own % 2, own // 2 % 2, own // 4
        self.pairs = devices // 8

    def block(self, weights):
        half = -(-weights.shape[1] // (2 * LANES)) * LANES
        padded = jnp.pad(weights, ((0, 0), (0, 2 * half - weights.shape[1])))
        mine = lax.dynamic_slice(padded, (0, half * self.x), (weights.shape[0], half))
        other = self.send(mine, target=lambda x, y, z, core: (x, y, z, 1 - core))
        return jnp.where(
            self.core == 0, jnp.concatenate([mine, other]), jnp.concatenate([other, mine])
        )

    def along(self, block):
        return [
            self.send(block, target=lambda x, y, z, core: (x, y, z ^ (2 * pair + core), core))
            for pair in range(self.pairs)
        ]

    def beside(self, first):
        second = self.send(
            first,
            target=lambda x, y, z, core: (x, 1 - y, z, core) if core else (x ^ 1, y, z, core),
        )
        return jnp.concatenate([first, second])

    def across(self, both):
        rest = self.send(
            both,
            target=lambda x, y, z, core: (x ^ 1, y, z, core) if core else (x, 1 - y, z, core),
        )
        return jnp.concatenate([both, rest])

    def swap(self, four):
        return self.send(four, target=lambda x, y, z, core: (x, y, z, 1 - core))

    def places(self, pairs, rows, half):
        found = []
        for parity in (self.core, 1 - self.core):
            for slot in range(4):
                for pair in pairs:
                    far_x = jnp.where(parity == 0, slot % 2, slot // 2)
                    far_y = jnp.where(parity == 0, slot // 2, slot % 2)
                    chip = 2 * (self.z ^ (2 * pair + parity)) + (self.y ^ far_y)
                    found += [rows * chip, half * (self.x ^ far_x)]
        return found


def tied(first, second):
    return lax.optimization_barrier((first, second))


def shards(
    clips,
    spatial_saved,
    hidden,
    temporal_out_grad,
    stream_grad,
    modulation,
    temporal_weights,
    spatial_weights,
):
    frames = lax.axis_size("seq")
    tokens, depth = hidden.shape[1:]
    width = temporal_out_grad.shape[2]
    patches = tokens // frames
    chips = frames // 2
    gain = 1.0 + modulation.reshape(1, depth)
    saved = spatial_saved.transpose(0, 1, 3, 2).reshape(3, HEADS, HD, tokens)
    mixed = jnp.concatenate([hidden, temporal_out_grad], axis=2).reshape(frames, patches, depth + width)
    if clips % 2 == 0 and chips >= 4 and chips & (chips - 1) == 0 and 2 * depth // frames % 16 == 0:
        gather = Gather(clips, frames)
        firsts = gather.along(gather.block(temporal_weights))
        small = gather.along(gather.block(spatial_weights))
        rows, half = firsts[0].shape
        places = [place for pair in range(len(firsts)) for place in gather.places([pair], rows, half)]
        small_places = gather.places(range(len(firsts)), 1, small[0].shape[1])
        places, small_places = (jnp.stack(p).astype(jnp.int32) for p in (places, small_places))
        (firsts, small, places, small_places, gain), mixed = tied(
            (firsts, small, places, small_places, gain), mixed
        )
        mixed = lax.all_to_all(mixed, "seq", split_axis=0, concat_axis=0, tiled=True)
        both = [gather.beside(first[None]) for first in firsts]
        small = gather.beside(jnp.stack(small))
        both[0], small = tied(both[0], small)
        four = [gather.across(block) for block in both]
        four[-1], mixed = tied(four[-1], mixed)
        pieces = [piece for block in four for piece in (block, gather.swap(block))]
        small = gather.across(small)
        small_pieces = [small, gather.swap(small)]
    else:
        mixed = lax.all_to_all(mixed, "seq", split_axis=0, concat_axis=0, tiled=True)
        places = small_places = jnp.zeros((2,), jnp.int32)
        pieces = [lax.all_gather(temporal_weights, "seq", axis=0, tiled=True)[None]]
        small_pieces = [lax.all_gather(spatial_weights, "seq", axis=0, tiled=True)[None]]
    branch = temporal(mixed.reshape(tokens, depth + width), gain, pieces, places, width, patches)
    attention_t, values, stream, weights = prepare(
        saved, stream_grad.reshape(tokens, depth), small_pieces, small_places, width
    )
    branch = lax.all_to_all(
        branch.reshape(frames, patches, depth), "seq", split_axis=0, concat_axis=0, tiled=True
    )
    hidden_grad, spatial_grad = spatial(
        attention_t,
        values,
        saved,
        stream,
        branch.reshape(tokens, depth),
        weights,
    )
    spatial_grad = spatial_grad.reshape(3, 1, width, tokens).transpose(0, 1, 3, 2)
    return (hidden_grad.reshape(1, tokens, depth), spatial_grad)


def solution(mesh):
    return jax.shard_map(
        functools.partial(shards, mesh.shape["clip"]),
        mesh=mesh,
        in_specs=(
            P(None, ("clip", "seq"), None, None),
            P(("clip", "seq"), None, None),
            P(("clip", "seq"), None, None),
            P(("clip", "seq"), None, None),
            P(),
            P("seq", None),
            P("seq", None),
        ),
        out_specs=(P(("clip", "seq"), None, None), P(None, ("clip", "seq"), None, None)),
        check_vma=False,
    )
```

```python
import functools
import math

import jax
import jax.numpy as jnp
from jax import lax
from jax.experimental import pallas as pl
from jax.experimental.pallas import tpu as pltpu
from jax.sharding import PartitionSpec as P

HEADS = 8
HD = 72
LANES = 128
PARTS = 2

epsilon = 1e-06
VMEM_LIMIT = 24 * 1024 * 1024


def window(head, width):
    low, high = head * HD, (head + 1) * HD
    start = low // LANES * LANES
    stop = min(-(-high // LANES) * LANES, width)
    return start, stop, low, high


def keep(block, start, low, high):
    lane = lax.broadcasted_iota(jnp.int32, block.shape, 1) + start
    return jnp.where((lane >= low) & (lane < high), block, jnp.zeros_like(block))


def dot_nt(a, b):
    return lax.dot_general(a, b, (((1,), (1,)), ((), ())), preferred_element_type=jnp.float32)


def dot_tn(a, b):
    return lax.dot_general(a, b, (((0,), (0,)), ((), ())), preferred_element_type=jnp.float32)


def dot_nn(a, b):
    return jnp.dot(a, b, preferred_element_type=jnp.float32)


def soft(scores_t, scale):
    top = jnp.max(scores_t, axis=0, keepdims=True)
    raised = jnp.exp2((scores_t - top) * (scale * math.log2(math.e)))
    return raised * (1.0 / jnp.sum(raised, axis=0, keepdims=True))


class Tiles:
    def __init__(self):
        self.sums = {}

    def add(self, start, part):
        for offset in range(0, part.shape[1], LANES):
            piece = part[:, offset : offset + LANES]
            key = start + offset
            self.sums[key] = self.sums[key] + piece if key in self.sums else piece

    def store(self, ref, base, width, scale, upto):
        for key in sorted(self.sums):
            stop = min(key + LANES, width)
            if stop <= upto:
                done = self.sums.pop(key)[:, : stop - key] * scale
                ref[:, base + key : base + stop] = done.astype(ref.dtype)


def head_grads(attention_t, query, keys, values, grad_o, start, low, high):
    rounded_t = attention_t.astype(jnp.bfloat16)
    spread_t = dot_nt(keep(values, start, low, high), grad_o)
    wide = rounded_t.astype(jnp.float32)
    delta = jnp.sum(wide * spread_t, axis=0, keepdims=True)
    dscore_t = (attention_t.astype(jnp.float32) * (spread_t - delta)).astype(jnp.bfloat16)
    return (
        dot_tn(dscore_t, keep(keys, start, low, high)),
        dot_nn(dscore_t, keep(query, start, low, high)),
        dot_nn(rounded_t, keep(grad_o, start, low, high)),
    )


def temporal_kernel(patches, count, place_ref, x_ref, gain_ref, *refs):
    pieces, refs = refs[:count], refs[count:]
    out_ref, bias_ref, proj_ref, keys_ref, grad_ref, gk_ref, held_ref, sems = refs
    tokens, depth = out_ref.shape
    width = keys_ref.shape[1]
    scale = 1.0 / math.sqrt(HD)
    copies = []
    for index, piece in enumerate(pieces):
        for slot in range(piece.shape[0]):
            rows, columns = piece.shape[1:]
            number = len(copies)
            if rows == depth:
                copies.append(pltpu.make_async_copy(piece.at[slot], held_ref, sems.at[number]))
                copies[-1].start()
                continue
            row = pl.multiple_of(place_ref[2 * number], rows)
            column = pl.multiple_of(place_ref[2 * number + 1], columns)
            copies.append(
                pltpu.make_async_copy(
                    piece.at[slot],
                    held_ref.at[pl.ds(row, rows), pl.ds(column, columns)],
                    sems.at[number],
                )
            )
            copies[-1].start()
    row = lax.broadcasted_iota(jnp.int32, (tokens, tokens), 0)
    column = lax.broadcasted_iota(jnp.int32, (tokens, tokens), 1)
    bias_ref[...] = jnp.where(lax.rem(row, patches) == lax.rem(column, patches), 0.0, -1e30)
    gain = gain_ref[...]
    widened = x_ref[:, :depth].astype(jnp.float32)
    centered = widened - jnp.mean(widened, axis=-1, keepdims=True)
    inverse = lax.rsqrt(jnp.mean(centered * centered, axis=-1, keepdims=True) + epsilon)
    normed = (centered * inverse * gain).astype(jnp.bfloat16)
    for copy in copies:
        copy.wait()
    proj_ref[...] = dot_nn(normed, held_ref[:, : 3 * width]).astype(jnp.bfloat16)
    keys_ref[...] = proj_ref[:, width : 2 * width]
    sums = [Tiles(), Tiles(), Tiles()]
    for head in range(HEADS):
        start, stop, low, high = window(head, width)
        query = proj_ref[:, start:stop]
        keys = keys_ref[:, start:stop]
        values = proj_ref[:, 2 * width + start : 2 * width + stop]
        grad_o = x_ref[:, depth + start : depth + stop]
        scores_t = dot_nt(keep(keys, start, low, high), query) + bias_ref[...]
        parts = head_grads(soft(scores_t, scale), query, keys, values, grad_o, start, low, high)
        for tiles, part in zip(sums, parts):
            tiles.add(start, part)
        upto = width if head == HEADS - 1 else high // LANES * LANES
        sums[0].store(grad_ref, 0, width, scale, upto)
        sums[1].store(gk_ref, 0, width, scale, upto)
        sums[2].store(grad_ref, 2 * width, width, 1.0, upto)
    grad_ref[:, width : 2 * width] = gk_ref[...]
    scaled = dot_nt(grad_ref[...], held_ref[:, : 3 * width]) * gain
    widened = x_ref[:, :depth].astype(jnp.float32)
    centered = widened - jnp.mean(widened, axis=-1, keepdims=True)
    normal_form = centered * inverse
    branch = inverse * (
        scaled
        - jnp.mean(scaled, axis=-1, keepdims=True)
        - normal_form * jnp.mean(scaled * normal_form, axis=-1, keepdims=True)
    )
    out_ref[...] = branch.astype(out_ref.dtype)


def temporal(mixed, gain, pieces, places, width, patches):
    tokens, depth = mixed.shape[0], gain.shape[1]
    held = max(2 * pieces[0].shape[2], 3 * width) if len(pieces) > 1 else pieces[0].shape[2]
    count = sum(piece.shape[0] for piece in pieces)
    return pl.pallas_call(
        functools.partial(temporal_kernel, patches, len(pieces)),
        out_shape=jax.ShapeDtypeStruct((tokens, depth), jnp.bfloat16),
        in_specs=[pl.BlockSpec(memory_space=pltpu.SMEM)]
        + [pl.BlockSpec(memory_space=pltpu.VMEM)] * 2
        + [pl.BlockSpec(memory_space=pl.ANY)] * len(pieces),
        out_specs=pl.BlockSpec(memory_space=pltpu.VMEM),
        scratch_shapes=[
            pltpu.VMEM((tokens, tokens), jnp.float32),
            pltpu.VMEM((tokens, 3 * width), jnp.bfloat16),
            pltpu.VMEM((tokens, width), jnp.bfloat16),
            pltpu.VMEM((tokens, 3 * width), jnp.bfloat16),
            pltpu.VMEM((tokens, width), jnp.bfloat16),
            pltpu.VMEM((depth, held), jnp.bfloat16),
            pltpu.SemaphoreType.DMA((count,)),
        ],
        compiler_params=pltpu.CompilerParams(vmem_limit_bytes=VMEM_LIMIT),
        cost_estimate=pl.CostEstimate(
            flops=12 * tokens * depth * width + 12 * HEADS * tokens * tokens * 2 * LANES,
            bytes_accessed=2 * (2 * tokens * 3 * width + 3 * depth * width),
            transcendentals=HEADS * tokens * tokens,
        ),
        name="temporal_backward",
    )(places, mixed, gain, *pieces)


def prepare_kernel(count, place_ref, saved_ref, stream_ref, *refs):
    pieces, refs = refs[:count], refs[count:]
    attention_refs, weights_refs = refs[:PARTS], refs[PARTS : 2 * PARTS]
    values_ref, held_stream_ref, held_ref, sems = refs[2 * PARTS :]
    copies = []
    for piece in pieces:
        for slot in range(piece.shape[0]):
            number = len(copies)
            if piece.shape[2] == held_ref.shape[2]:
                target = held_ref.at[slot]
            else:
                column = pl.multiple_of(place_ref[2 * number + 1], piece.shape[2])
                target = held_ref.at[place_ref[2 * number], :, pl.ds(column, piece.shape[2])]
            copies.append(pltpu.make_async_copy(piece.at[slot], target, sems.at[number]))
            copies[-1].start()
    held_stream_ref[...] = stream_ref[...]
    for head in range(HEADS):
        scores_t = dot_tn(saved_ref[1, head], saved_ref[0, head])
        part = attention_refs[head * PARTS // HEADS]
        part[head % (HEADS // PARTS)] = soft(scores_t, 1.0 / math.sqrt(HD)).astype(part.dtype)
        values_ref[head] = saved_ref[2, head].astype(jnp.float32).T.astype(values_ref.dtype)
    for copy in copies:
        copy.wait()
    blocks = [held_ref[chip].astype(jnp.float32) for chip in range(held_ref.shape[0])]
    joined = jnp.concatenate(blocks, axis=0)
    for index, part in enumerate(weights_refs):
        rows, depth = part.shape
        part[...] = joined[index * rows : (index + 1) * rows, :depth].astype(part.dtype)


def prepare(saved, stream, pieces, places, width):
    tokens, depth = stream.shape
    rows = pieces[0].shape[1]
    held = max(depth, pieces[0].shape[2] * (1 if len(pieces) == 1 else 2))
    count = sum(piece.shape[0] for piece in pieces)
    return pl.pallas_call(
        functools.partial(prepare_kernel, len(pieces)),
        out_shape=(jax.ShapeDtypeStruct((HEADS // PARTS, tokens, tokens), jnp.bfloat16),) * PARTS
        + (jax.ShapeDtypeStruct((width // PARTS, depth), jnp.bfloat16),) * PARTS
        + (
            jax.ShapeDtypeStruct((HEADS, tokens, HD), jnp.bfloat16),
            jax.ShapeDtypeStruct((tokens, depth), jnp.bfloat16),
        ),
        in_specs=[pl.BlockSpec(memory_space=pltpu.SMEM)]
        + [pl.BlockSpec(memory_space=pltpu.VMEM)] * 2
        + [pl.BlockSpec(memory_space=pl.ANY)] * len(pieces),
        out_specs=(pl.BlockSpec(memory_space=pltpu.VMEM),) * (2 * PARTS + 2),
        scratch_shapes=[
            pltpu.VMEM((width // rows, rows, held), jnp.bfloat16),
            pltpu.SemaphoreType.DMA((count,)),
        ],
        compiler_params=pltpu.CompilerParams(vmem_limit_bytes=VMEM_LIMIT),
        cost_estimate=pl.CostEstimate(
            flops=2 * HEADS * tokens * tokens * 2 * LANES,
            bytes_accessed=2 * (4 * HEADS * tokens * HD + HEADS * tokens * tokens),
            transcendentals=HEADS * tokens * tokens,
        ),
        name="spatial_prepare",
    )(places, saved, stream, *pieces)


def spatial_kernel(values_ref, saved_ref, stream_ref, branch_ref, *refs):
    attention_refs, w_refs, (hidden_ref, out_ref) = refs[:PARTS], refs[PARTS:-2], refs[-2:]
    scale = 1.0 / math.sqrt(HD)
    hidden_grad = (
        stream_ref[...].astype(jnp.float32) + branch_ref[...].astype(jnp.float32)
    ).astype(jnp.bfloat16)
    hidden_ref[...] = hidden_grad
    grad_all = jnp.concatenate([dot_nt(w_ref[...], hidden_grad) for w_ref in w_refs], axis=0)
    for head in range(HEADS):
        grad_o = grad_all[head * HD : (head + 1) * HD].astype(jnp.bfloat16)
        rounded_t = attention_refs[head * PARTS // HEADS][head % (HEADS // PARTS)]
        wide = rounded_t.astype(jnp.float32)
        spread_t = dot_nn(values_ref[head], grad_o)
        delta = jnp.sum(wide * spread_t, axis=0, keepdims=True)
        dscore_t = (wide * (spread_t - delta)).astype(jnp.bfloat16)
        out_ref[0, head] = (dot_nn(saved_ref[1, head], dscore_t) * scale).astype(out_ref.dtype)
        out_ref[1, head] = (dot_nt(saved_ref[0, head], dscore_t) * scale).astype(out_ref.dtype)
        out_ref[2, head] = dot_nt(grad_o, rounded_t).astype(out_ref.dtype)


def spatial(attention_t, values, saved, stream, branch, weights):
    tokens, depth = stream.shape
    width = HEADS * HD
    return pl.pallas_call(
        spatial_kernel,
        out_shape=(
            jax.ShapeDtypeStruct((tokens, depth), jnp.bfloat16),
            jax.ShapeDtypeStruct((3, HEADS, HD, tokens), jnp.bfloat16),
        ),
        compiler_params=pltpu.CompilerParams(vmem_limit_bytes=VMEM_LIMIT),
        cost_estimate=pl.CostEstimate(
            flops=2 * tokens * depth * width + 10 * HEADS * tokens * tokens * 2 * LANES,
            bytes_accessed=2 * (3 * tokens * depth + depth * width + 6 * tokens * width),
            transcendentals=0,
        ),
        name="spatial_backward",
    )(values, saved, stream, branch, *attention_t, *weights)


def moved(block, clips, devices, target):
    pairs = []
    for clip in range(clips):
        for own in range(devices):
            x, y, z, core = target(clip, own // 2 % 2, own // 4, own % 2)
            pairs.append((clip * devices + own, x * devices + (2 * z + y) * 2 + core))
    return lax.ppermute(block, ("clip", "seq"), pairs)


class Gather:
    def __init__(self, clips, devices):
        self.send = functools.partial(moved, clips=clips, devices=devices)
        clip, own = lax.axis_index("clip"), lax.axis_index("seq")
        self.x, self.core, self.y, self.z = clip % 2, own % 2, own // 2 % 2, own // 4
        self.pairs = devices // 8

    def block(self, weights):
        half = -(-weights.shape[1] // (2 * LANES)) * LANES
        padded = jnp.pad(weights, ((0, 0), (0, 2 * half - weights.shape[1])))
        mine = lax.dynamic_slice(padded, (0, half * self.x), (weights.shape[0], half))
        other = self.send(mine, target=lambda x, y, z, core: (x, y, z, 1 - core))
        return jnp.where(
            self.core == 0, jnp.concatenate([mine, other]), jnp.concatenate([other, mine])
        )

    def along(self, block):
        return [
            self.send(block, target=lambda x, y, z, core: (x, y, z ^ (2 * pair + core), core))
            for pair in range(self.pairs)
        ]

    def beside(self, first):
        second = self.send(
            first,
            target=lambda x, y, z, core: (x, 1 - y, z, core) if core else (x ^ 1, y, z, core),
        )
        return first, second

    def across(self, both):
        rest = self.send(
            both,
            target=lambda x, y, z, core: (x ^ 1, y, z, core) if core else (x, 1 - y, z, core),
        )
        return jnp.concatenate([both, rest])

    def swap(self, four):
        return self.send(four, target=lambda x, y, z, core: (x, y, z, 1 - core))

    def places(self, pairs, rows, half):
        found = []
        for parity in (self.core, 1 - self.core):
            for slot in range(4):
                for pair in pairs:
                    far_x = jnp.where(parity == 0, slot % 2, slot // 2)
                    far_y = jnp.where(parity == 0, slot // 2, slot % 2)
                    chip = 2 * (self.z ^ (2 * pair + parity)) + (self.y ^ far_y)
                    found += [rows * chip, half * (self.x ^ far_x)]
        return found


def tied(first, second):
    return lax.optimization_barrier((first, second))


def shards(
    clips,
    spatial_saved,
    hidden,
    temporal_out_grad,
    stream_grad,
    modulation,
    temporal_weights,
    spatial_weights,
):
    frames = lax.axis_size("seq")
    tokens, depth = hidden.shape[1:]
    width = temporal_out_grad.shape[2]
    patches = tokens // frames
    chips = frames // 2
    gain = 1.0 + modulation.reshape(1, depth)
    saved = spatial_saved.transpose(0, 1, 3, 2).reshape(3, HEADS, HD, tokens)
    mixed = jnp.concatenate([hidden, temporal_out_grad], axis=2).reshape(frames, patches, depth + width)
    if clips % 2 == 0 and chips >= 4 and chips & (chips - 1) == 0 and 2 * depth // frames % 16 == 0:
        gather = Gather(clips, frames)
        block = gather.block(temporal_weights)
        firsts = gather.along(block)
        rows, half = firsts[0].shape
        small_block = gather.block(spatial_weights)
        places = [place for pair in range(len(firsts)) for place in gather.places([pair], rows, half)]
        small_places = gather.places(range(len(firsts)), 1, small_block.shape[1])
        places, small_places = (jnp.stack(p).astype(jnp.int32) for p in (places, small_places))
        both = [jnp.concatenate(gather.beside(firsts[0][None]))]
        (both[0], firsts, small_block, places, small_places, gain), mixed = tied(
            (both[0], firsts, small_block, places, small_places, gain), mixed
        )
        mixed = lax.all_to_all(mixed, "seq", split_axis=0, concat_axis=0, tiled=True)
        both += [jnp.concatenate(gather.beside(first[None])) for first in firsts[1:]]
        small = jnp.stack(gather.along(small_block))
        four = [gather.across(block) for block in both]
        (four[-1], small), mixed = tied((four[-1], small), mixed)
        pieces = [piece for block in four for piece in (block, gather.swap(block))]
        small = gather.beside(small)
    else:
        mixed = lax.all_to_all(mixed, "seq", split_axis=0, concat_axis=0, tiled=True)
        places = small_places = jnp.zeros((2,), jnp.int32)
        pieces = [lax.all_gather(temporal_weights, "seq", axis=0, tiled=True)[None]]
        gather, small_pieces = None, [lax.all_gather(spatial_weights, "seq", axis=0, tiled=True)[None]]
    branch = temporal(mixed.reshape(tokens, depth + width), gain, pieces, places, width, patches)
    if gather:
        small, branch = tied(small, branch)
        small = gather.across(jnp.concatenate(small))
        small_pieces = [small, gather.swap(small)]
    *parts, values, stream = prepare(
        saved, stream_grad.reshape(tokens, depth), small_pieces, small_places, width
    )
    branch = lax.all_to_all(
        branch.reshape(frames, patches, depth), "seq", split_axis=0, concat_axis=0, tiled=True
    )
    hidden_grad, spatial_grad = spatial(
        parts[:PARTS], values, saved, stream, branch.reshape(tokens, depth), parts[PARTS:]
    )
    spatial_grad = spatial_grad.reshape(3, 1, width, tokens).transpose(0, 1, 3, 2)
    return (hidden_grad.reshape(1, tokens, depth), spatial_grad)


def solution(mesh):
    return jax.shard_map(
        functools.partial(shards, mesh.shape["clip"]),
        mesh=mesh,
        in_specs=(
            P(None, ("clip", "seq"), None, None),
            P(("clip", "seq"), None, None),
            P(("clip", "seq"), None, None),
            P(("clip", "seq"), None, None),
            P(),
            P("seq", None),
            P("seq", None),
        ),
        out_specs=(P(("clip", "seq"), None, None), P(None, ("clip", "seq"), None, None)),
        check_vma=False,
    )
```

```python
import functools
import math

import jax
import jax.numpy as jnp
from jax import lax
from jax.experimental import pallas as pl
from jax.experimental.pallas import tpu as pltpu
from jax.sharding import PartitionSpec as P

HEADS = 8
HD = 72
LANES = 128
PARTS = 2

epsilon = 1e-06
VMEM_LIMIT = 24 * 1024 * 1024


def window(head, width):
    low, high = head * HD, (head + 1) * HD
    start = low // LANES * LANES
    stop = min(-(-high // LANES) * LANES, width)
    return start, stop, low, high


def keep(block, start, low, high):
    lane = lax.broadcasted_iota(jnp.int32, block.shape, 1) + start
    return jnp.where((lane >= low) & (lane < high), block, jnp.zeros_like(block))


def dot_nt(a, b):
    return lax.dot_general(a, b, (((1,), (1,)), ((), ())), preferred_element_type=jnp.float32)


def dot_tn(a, b):
    return lax.dot_general(a, b, (((0,), (0,)), ((), ())), preferred_element_type=jnp.float32)


def dot_nn(a, b):
    return jnp.dot(a, b, preferred_element_type=jnp.float32)


def soft(scores_t, scale):
    top = jnp.max(scores_t, axis=0, keepdims=True)
    raised = jnp.exp2((scores_t - top) * (scale * math.log2(math.e)))
    return raised * (1.0 / jnp.sum(raised, axis=0, keepdims=True))


class Tiles:
    def __init__(self):
        self.sums = {}

    def add(self, start, part):
        for offset in range(0, part.shape[1], LANES):
            piece = part[:, offset : offset + LANES]
            key = start + offset
            self.sums[key] = self.sums[key] + piece if key in self.sums else piece

    def store(self, ref, base, width, scale, upto):
        for key in sorted(self.sums):
            stop = min(key + LANES, width)
            if stop <= upto:
                done = self.sums.pop(key)[:, : stop - key] * scale
                ref[:, base + key : base + stop] = done.astype(ref.dtype)


def head_grads(attention_t, query, keys, values, grad_o, start, low, high):
    rounded_t = attention_t.astype(jnp.bfloat16)
    spread_t = dot_nt(keep(values, start, low, high), grad_o)
    wide = rounded_t.astype(jnp.float32)
    delta = jnp.sum(wide * spread_t, axis=0, keepdims=True)
    dscore_t = (attention_t.astype(jnp.float32) * (spread_t - delta)).astype(jnp.bfloat16)
    return (
        dot_tn(dscore_t, keep(keys, start, low, high)),
        dot_nn(dscore_t, keep(query, start, low, high)),
        dot_nn(rounded_t, keep(grad_o, start, low, high)),
    )


def temporal_kernel(patches, count, place_ref, x_ref, gain_ref, *refs):
    pieces, refs = refs[:count], refs[count:]
    out_ref, bias_ref, proj_ref, keys_ref, grad_ref, gk_ref, held_ref, sems = refs
    tokens, depth = out_ref.shape
    width = keys_ref.shape[1]
    scale = 1.0 / math.sqrt(HD)
    copies = []
    for index, piece in enumerate(pieces):
        for slot in range(piece.shape[0]):
            rows, columns = piece.shape[1:]
            number = len(copies)
            if rows == depth:
                copies.append(pltpu.make_async_copy(piece.at[slot], held_ref, sems.at[number]))
                copies[-1].start()
                continue
            row = pl.multiple_of(place_ref[2 * number], rows)
            column = pl.multiple_of(place_ref[2 * number + 1], columns)
            copies.append(
                pltpu.make_async_copy(
                    piece.at[slot],
                    held_ref.at[pl.ds(row, rows), pl.ds(column, columns)],
                    sems.at[number],
                )
            )
            copies[-1].start()
    row = lax.broadcasted_iota(jnp.int32, (tokens, tokens), 0)
    column = lax.broadcasted_iota(jnp.int32, (tokens, tokens), 1)
    bias_ref[...] = jnp.where(lax.rem(row, patches) == lax.rem(column, patches), 0.0, -1e30)
    gain = gain_ref[...]
    widened = x_ref[:, :depth].astype(jnp.float32)
    centered = widened - jnp.mean(widened, axis=-1, keepdims=True)
    inverse = lax.rsqrt(jnp.mean(centered * centered, axis=-1, keepdims=True) + epsilon)
    normed = (centered * inverse * gain).astype(jnp.bfloat16)
    for copy in copies:
        copy.wait()
    proj_ref[...] = dot_nn(normed, held_ref[:, : 3 * width]).astype(jnp.bfloat16)
    keys_ref[...] = proj_ref[:, width : 2 * width]
    sums = [Tiles(), Tiles(), Tiles()]
    for head in range(HEADS):
        start, stop, low, high = window(head, width)
        query = proj_ref[:, start:stop]
        keys = keys_ref[:, start:stop]
        values = proj_ref[:, 2 * width + start : 2 * width + stop]
        grad_o = x_ref[:, depth + start : depth + stop]
        scores_t = dot_nt(keep(keys, start, low, high), query) + bias_ref[...]
        parts = head_grads(soft(scores_t, scale), query, keys, values, grad_o, start, low, high)
        for tiles, part in zip(sums, parts):
            tiles.add(start, part)
        upto = width if head == HEADS - 1 else high // LANES * LANES
        sums[0].store(grad_ref, 0, width, scale, upto)
        sums[1].store(gk_ref, 0, width, scale, upto)
        sums[2].store(grad_ref, 2 * width, width, 1.0, upto)
    grad_ref[:, width : 2 * width] = gk_ref[...]
    scaled = dot_nt(grad_ref[...], held_ref[:, : 3 * width]) * gain
    widened = x_ref[:, :depth].astype(jnp.float32)
    centered = widened - jnp.mean(widened, axis=-1, keepdims=True)
    normal_form = centered * inverse
    branch = inverse * (
        scaled
        - jnp.mean(scaled, axis=-1, keepdims=True)
        - normal_form * jnp.mean(scaled * normal_form, axis=-1, keepdims=True)
    )
    out_ref[...] = branch.astype(out_ref.dtype)


def temporal(mixed, gain, pieces, places, width, patches):
    tokens, depth = mixed.shape[0], gain.shape[1]
    held = max(2 * pieces[0].shape[2], 3 * width) if len(pieces) > 1 else pieces[0].shape[2]
    count = sum(piece.shape[0] for piece in pieces)
    return pl.pallas_call(
        functools.partial(temporal_kernel, patches, len(pieces)),
        out_shape=jax.ShapeDtypeStruct((tokens, depth), jnp.bfloat16),
        in_specs=[pl.BlockSpec(memory_space=pltpu.SMEM)]
        + [pl.BlockSpec(memory_space=pltpu.VMEM)] * 2
        + [pl.BlockSpec(memory_space=pl.ANY)] * len(pieces),
        out_specs=pl.BlockSpec(memory_space=pltpu.VMEM),
        scratch_shapes=[
            pltpu.VMEM((tokens, tokens), jnp.float32),
            pltpu.VMEM((tokens, 3 * width), jnp.bfloat16),
            pltpu.VMEM((tokens, width), jnp.bfloat16),
            pltpu.VMEM((tokens, 3 * width), jnp.bfloat16),
            pltpu.VMEM((tokens, width), jnp.bfloat16),
            pltpu.VMEM((depth, held), jnp.bfloat16),
            pltpu.SemaphoreType.DMA((count,)),
        ],
        compiler_params=pltpu.CompilerParams(vmem_limit_bytes=VMEM_LIMIT),
        cost_estimate=pl.CostEstimate(
            flops=12 * tokens * depth * width + 12 * HEADS * tokens * tokens * 2 * LANES,
            bytes_accessed=2 * (2 * tokens * 3 * width + 3 * depth * width),
            transcendentals=HEADS * tokens * tokens,
        ),
        name="temporal_backward",
    )(places, mixed, gain, *pieces)


def prepare_kernel(count, place_ref, saved_ref, stream_ref, *refs):
    pieces, refs = refs[:count], refs[count:]
    attention_refs, weights_refs = refs[:PARTS], refs[PARTS : 2 * PARTS]
    values_ref, held_stream_ref, held_ref, sems = refs[2 * PARTS :]
    copies = []
    for piece in pieces:
        for slot in range(piece.shape[0]):
            number = len(copies)
            if piece.shape[2] == held_ref.shape[2]:
                target = held_ref.at[slot]
            else:
                column = pl.multiple_of(place_ref[2 * number + 1], piece.shape[2])
                target = held_ref.at[place_ref[2 * number], :, pl.ds(column, piece.shape[2])]
            copies.append(pltpu.make_async_copy(piece.at[slot], target, sems.at[number]))
            copies[-1].start()
    held_stream_ref[...] = stream_ref[...]
    for head in range(HEADS):
        scores_t = dot_tn(saved_ref[1, head], saved_ref[0, head])
        part = attention_refs[head * PARTS // HEADS]
        part[head % (HEADS // PARTS)] = soft(scores_t, 1.0 / math.sqrt(HD)).astype(part.dtype)
        values_ref[head] = saved_ref[2, head].astype(jnp.float32).T.astype(values_ref.dtype)
    for copy in copies:
        copy.wait()
    blocks = [held_ref[chip].astype(jnp.float32) for chip in range(held_ref.shape[0])]
    joined = jnp.concatenate(blocks, axis=0)
    for index, part in enumerate(weights_refs):
        rows, depth = part.shape
        part[...] = joined[index * rows : (index + 1) * rows, :depth].astype(part.dtype)


def prepare(saved, stream, pieces, places, width):
    tokens, depth = stream.shape
    rows = pieces[0].shape[1]
    held = max(depth, pieces[0].shape[2] * (1 if len(pieces) == 1 else 2))
    count = sum(piece.shape[0] for piece in pieces)
    return pl.pallas_call(
        functools.partial(prepare_kernel, len(pieces)),
        out_shape=(jax.ShapeDtypeStruct((HEADS // PARTS, tokens, tokens), jnp.bfloat16),) * PARTS
        + (jax.ShapeDtypeStruct((width // PARTS, depth), jnp.bfloat16),) * PARTS
        + (
            jax.ShapeDtypeStruct((HEADS, tokens, HD), jnp.bfloat16),
            jax.ShapeDtypeStruct((tokens, depth), jnp.bfloat16),
        ),
        in_specs=[pl.BlockSpec(memory_space=pltpu.SMEM)]
        + [pl.BlockSpec(memory_space=pltpu.VMEM)] * 2
        + [pl.BlockSpec(memory_space=pl.ANY)] * len(pieces),
        out_specs=(pl.BlockSpec(memory_space=pltpu.VMEM),) * (2 * PARTS + 2),
        scratch_shapes=[
            pltpu.VMEM((width // rows, rows, held), jnp.bfloat16),
            pltpu.SemaphoreType.DMA((count,)),
        ],
        compiler_params=pltpu.CompilerParams(vmem_limit_bytes=VMEM_LIMIT),
        cost_estimate=pl.CostEstimate(
            flops=2 * HEADS * tokens * tokens * 2 * LANES,
            bytes_accessed=2 * (4 * HEADS * tokens * HD + HEADS * tokens * tokens),
            transcendentals=HEADS * tokens * tokens,
        ),
        name="spatial_prepare",
    )(places, saved, stream, *pieces)


def spatial_kernel(values_ref, saved_ref, stream_ref, branch_ref, *refs):
    attention_refs, w_refs, (hidden_ref, out_ref) = refs[:PARTS], refs[PARTS:-2], refs[-2:]
    scale = 1.0 / math.sqrt(HD)
    hidden_grad = (
        stream_ref[...].astype(jnp.float32) + branch_ref[...].astype(jnp.float32)
    ).astype(jnp.bfloat16)
    hidden_ref[...] = hidden_grad
    grad_all = jnp.concatenate([dot_nt(w_ref[...], hidden_grad) for w_ref in w_refs], axis=0)
    for head in range(HEADS):
        grad_o = grad_all[head * HD : (head + 1) * HD].astype(jnp.bfloat16)
        rounded_t = attention_refs[head * PARTS // HEADS][head % (HEADS // PARTS)]
        wide = rounded_t.astype(jnp.float32)
        spread_t = dot_nn(values_ref[head], grad_o)
        delta = jnp.sum(wide * spread_t, axis=0, keepdims=True)
        dscore_t = (wide * (spread_t - delta)).astype(jnp.bfloat16)
        out_ref[0, head] = (dot_nn(saved_ref[1, head], dscore_t) * scale).astype(out_ref.dtype)
        out_ref[1, head] = (dot_nt(saved_ref[0, head], dscore_t) * scale).astype(out_ref.dtype)
        out_ref[2, head] = dot_nt(grad_o, rounded_t).astype(out_ref.dtype)


def spatial(attention_t, values, saved, stream, branch, weights):
    tokens, depth = stream.shape
    width = HEADS * HD
    return pl.pallas_call(
        spatial_kernel,
        out_shape=(
            jax.ShapeDtypeStruct((tokens, depth), jnp.bfloat16),
            jax.ShapeDtypeStruct((3, HEADS, HD, tokens), jnp.bfloat16),
        ),
        compiler_params=pltpu.CompilerParams(vmem_limit_bytes=VMEM_LIMIT),
        cost_estimate=pl.CostEstimate(
            flops=2 * tokens * depth * width + 10 * HEADS * tokens * tokens * 2 * LANES,
            bytes_accessed=2 * (3 * tokens * depth + depth * width + 6 * tokens * width),
            transcendentals=0,
        ),
        name="spatial_backward",
    )(values, saved, stream, branch, *attention_t, *weights)


def moved(block, clips, devices, target):
    pairs = []
    for clip in range(clips):
        for own in range(devices):
            x, y, z, core = target(clip, own // 2 % 2, own // 4, own % 2)
            pairs.append((clip * devices + own, x * devices + (2 * z + y) * 2 + core))
    return lax.ppermute(block, ("clip", "seq"), pairs)


def half_of(columns):
    return -(-columns // (2 * LANES)) * LANES


class Gather:
    def __init__(self, clips, devices):
        self.send = functools.partial(moved, clips=clips, devices=devices)
        clip, own = lax.axis_index("clip"), lax.axis_index("seq")
        self.x, self.core, self.y, self.z = clip % 2, own % 2, own // 2 % 2, own // 4
        self.pairs = devices // 8

    def block(self, weights):
        other = self.send(weights, target=lambda x, y, z, core: (x, y, z, 1 - core))
        rows = jnp.where(
            self.core == 0,
            jnp.concatenate([weights, other]),
            jnp.concatenate([other, weights]),
        )
        half = half_of(weights.shape[1])
        padded = jnp.pad(rows, ((0, 0), (0, 2 * half - weights.shape[1])))
        return jnp.where(self.x == 0, padded[:, :half], padded[:, half:])

    def along(self, block, late=None):
        return [
            self.send(
                block if pair or late is None else late,
                target=lambda x, y, z, core: (x, y, z ^ (2 * pair + core), core),
            )
            for pair in range(self.pairs)
        ]

    def beside(self, first):
        second = self.send(
            first,
            target=lambda x, y, z, core: (x, 1 - y, z, core) if core else (x ^ 1, y, z, core),
        )
        return first, second

    def across(self, both):
        rest = self.send(
            both,
            target=lambda x, y, z, core: (x ^ 1, y, z, core) if core else (x, 1 - y, z, core),
        )
        return jnp.concatenate([both, rest])

    def swap(self, four):
        return self.send(four, target=lambda x, y, z, core: (x, y, z, 1 - core))

    def places(self, pairs, rows, half):
        found = []
        for parity in (self.core, 1 - self.core):
            for slot in range(4):
                for pair in pairs:
                    far_x = jnp.where(parity == 0, slot % 2, slot // 2)
                    far_y = jnp.where(parity == 0, slot // 2, slot % 2)
                    chip = 2 * (self.z ^ (2 * pair + parity)) + (self.y ^ far_y)
                    found += [rows * chip, half * (self.x ^ far_x)]
        return found


def tied(first, second):
    return lax.optimization_barrier((first, second))


def shards(
    clips,
    spatial_saved,
    hidden,
    temporal_out_grad,
    stream_grad,
    modulation,
    temporal_weights,
    spatial_weights,
):
    frames = lax.axis_size("seq")
    tokens, depth = hidden.shape[1:]
    width = temporal_out_grad.shape[2]
    patches = tokens // frames
    chips = frames // 2
    gain = 1.0 + modulation.reshape(1, depth)
    saved = spatial_saved.transpose(0, 1, 3, 2).reshape(3, HEADS, HD, tokens)
    mixed = jnp.concatenate([hidden, temporal_out_grad], axis=2).reshape(frames, patches, depth + width)
    if clips % 2 == 0 and chips >= 4 and chips & (chips - 1) == 0 and 2 * depth // frames % 16 == 0:
        gather = Gather(clips, frames)
        block = gather.block(temporal_weights)
        late, mixed = tied(block, mixed)
        firsts = gather.along(block, late)
        rows, half = firsts[0].shape
        places = [place for pair in range(len(firsts)) for place in gather.places([pair], rows, half)]
        small_places = gather.places(range(len(firsts)), 1, half_of(depth))
        places, small_places = (jnp.stack(p).astype(jnp.int32) for p in (places, small_places))
        both = [jnp.concatenate(gather.beside(firsts[0][None]))]
        (both[0], firsts, spatial_weights, places, small_places, gain), mixed = tied(
            (both[0], firsts, spatial_weights, places, small_places, gain), mixed
        )
        mixed = lax.all_to_all(mixed, "seq", split_axis=0, concat_axis=0, tiled=True)
        both += [jnp.concatenate(gather.beside(first[None])) for first in firsts[1:]]
        small = jnp.stack(gather.along(gather.block(spatial_weights)))
        four = [gather.across(block) for block in both]
        (four[-1], small), mixed = tied((four[-1], small), mixed)
        pieces = [piece for block in four for piece in (block, gather.swap(block))]
        small = gather.beside(small)
    else:
        mixed = lax.all_to_all(mixed, "seq", split_axis=0, concat_axis=0, tiled=True)
        places = small_places = jnp.zeros((2,), jnp.int32)
        pieces = [lax.all_gather(temporal_weights, "seq", axis=0, tiled=True)[None]]
        gather, small_pieces = None, [lax.all_gather(spatial_weights, "seq", axis=0, tiled=True)[None]]
    branch = temporal(mixed.reshape(tokens, depth + width), gain, pieces, places, width, patches)
    if gather:
        small, branch = tied(small, branch)
        small = gather.across(jnp.concatenate(small))
        small_pieces = [small, gather.swap(small)]
    *parts, values, stream = prepare(
        saved, stream_grad.reshape(tokens, depth), small_pieces, small_places, width
    )
    branch = lax.all_to_all(
        branch.reshape(frames, patches, depth), "seq", split_axis=0, concat_axis=0, tiled=True
    )
    hidden_grad, spatial_grad = spatial(
        parts[:PARTS], values, saved, stream, branch.reshape(tokens, depth), parts[PARTS:]
    )
    spatial_grad = spatial_grad.reshape(3, 1, width, tokens).transpose(0, 1, 3, 2)
    return (hidden_grad.reshape(1, tokens, depth), spatial_grad)


def solution(mesh):
    return jax.shard_map(
        functools.partial(shards, mesh.shape["clip"]),
        mesh=mesh,
        in_specs=(
            P(None, ("clip", "seq"), None, None),
            P(("clip", "seq"), None, None),
            P(("clip", "seq"), None, None),
            P(("clip", "seq"), None, None),
            P(),
            P("seq", None),
            P("seq", None),
        ),
        out_specs=(P(("clip", "seq"), None, None), P(None, ("clip", "seq"), None, None)),
        check_vma=False,
    )
```

```python
import functools
import math

import jax
import jax.numpy as jnp
from jax import lax
from jax.experimental import pallas as pl
from jax.experimental.pallas import tpu as pltpu
from jax.sharding import PartitionSpec as P

HEADS = 8
HD = 72
LANES = 128
PARTS = 2

epsilon = 1e-06
VMEM_LIMIT = 24 * 1024 * 1024


def window(head, width):
    low, high = head * HD, (head + 1) * HD
    start = low // LANES * LANES
    stop = min(-(-high // LANES) * LANES, width)
    return start, stop, low, high


def keep(block, start, low, high):
    lane = lax.broadcasted_iota(jnp.int32, block.shape, 1) + start
    return jnp.where((lane >= low) & (lane < high), block, jnp.zeros_like(block))


def dot_nt(a, b):
    return lax.dot_general(a, b, (((1,), (1,)), ((), ())), preferred_element_type=jnp.float32)


def dot_tn(a, b):
    return lax.dot_general(a, b, (((0,), (0,)), ((), ())), preferred_element_type=jnp.float32)


def dot_nn(a, b):
    return jnp.dot(a, b, preferred_element_type=jnp.float32)


def soft(scores_t, scale):
    top = jnp.max(scores_t, axis=0, keepdims=True)
    raised = jnp.exp2((scores_t - top) * (scale * math.log2(math.e)))
    return raised * (1.0 / jnp.sum(raised, axis=0, keepdims=True))


class Tiles:
    def __init__(self):
        self.sums = {}

    def add(self, start, part):
        for offset in range(0, part.shape[1], LANES):
            piece = part[:, offset : offset + LANES]
            key = start + offset
            self.sums[key] = self.sums[key] + piece if key in self.sums else piece

    def store(self, ref, base, width, scale, upto):
        for key in sorted(self.sums):
            stop = min(key + LANES, width)
            if stop <= upto:
                done = self.sums.pop(key)[:, : stop - key] * scale
                ref[:, base + key : base + stop] = done.astype(ref.dtype)


def head_grads(attention_t, query, keys, values, grad_o, start, low, high):
    rounded_t = attention_t.astype(jnp.bfloat16)
    spread_t = dot_nt(keep(values, start, low, high), grad_o)
    wide = rounded_t.astype(jnp.float32)
    delta = jnp.sum(wide * spread_t, axis=0, keepdims=True)
    dscore_t = (attention_t.astype(jnp.float32) * (spread_t - delta)).astype(jnp.bfloat16)
    return (
        dot_tn(dscore_t, keep(keys, start, low, high)),
        dot_nn(dscore_t, keep(query, start, low, high)),
        dot_nn(rounded_t, keep(grad_o, start, low, high)),
    )


def temporal_kernel(patches, count, place_ref, x_ref, gain_ref, *refs):
    pieces, refs = refs[:count], refs[count:]
    out_ref, bias_ref, proj_ref, keys_ref, grad_ref, gk_ref, held_ref, sems = refs
    tokens, depth = out_ref.shape
    width = keys_ref.shape[1]
    scale = 1.0 / math.sqrt(HD)
    copies = []
    for index, piece in enumerate(pieces):
        for slot in range(piece.shape[0]):
            rows, columns = piece.shape[1:]
            number = len(copies)
            if rows == depth:
                copies.append(pltpu.make_async_copy(piece.at[slot], held_ref, sems.at[number]))
                copies[-1].start()
                continue
            row = pl.multiple_of(place_ref[2 * number], rows)
            column = pl.multiple_of(place_ref[2 * number + 1], columns)
            copies.append(
                pltpu.make_async_copy(
                    piece.at[slot],
                    held_ref.at[pl.ds(row, rows), pl.ds(column, columns)],
                    sems.at[number],
                )
            )
            copies[-1].start()
    row = lax.broadcasted_iota(jnp.int32, (tokens, tokens), 0)
    column = lax.broadcasted_iota(jnp.int32, (tokens, tokens), 1)
    bias_ref[...] = jnp.where(lax.rem(row, patches) == lax.rem(column, patches), 0.0, -1e30)
    gain = gain_ref[...]
    widened = x_ref[:, :depth].astype(jnp.float32)
    centered = widened - jnp.mean(widened, axis=-1, keepdims=True)
    inverse = lax.rsqrt(jnp.mean(centered * centered, axis=-1, keepdims=True) + epsilon)
    normed = (centered * inverse * gain).astype(jnp.bfloat16)
    for copy in copies:
        copy.wait()
    proj_ref[...] = dot_nn(normed, held_ref[:, : 3 * width]).astype(jnp.bfloat16)
    keys_ref[...] = proj_ref[:, width : 2 * width]
    sums = [Tiles(), Tiles(), Tiles()]
    for head in range(HEADS):
        start, stop, low, high = window(head, width)
        query = proj_ref[:, start:stop]
        keys = keys_ref[:, start:stop]
        values = proj_ref[:, 2 * width + start : 2 * width + stop]
        grad_o = x_ref[:, depth + start : depth + stop]
        scores_t = dot_nt(keep(keys, start, low, high), query) + bias_ref[...]
        parts = head_grads(soft(scores_t, scale), query, keys, values, grad_o, start, low, high)
        for tiles, part in zip(sums, parts):
            tiles.add(start, part)
        upto = width if head == HEADS - 1 else high // LANES * LANES
        sums[0].store(grad_ref, 0, width, scale, upto)
        sums[1].store(gk_ref, 0, width, scale, upto)
        sums[2].store(grad_ref, 2 * width, width, 1.0, upto)
    grad_ref[:, width : 2 * width] = gk_ref[...]
    scaled = dot_nt(grad_ref[...], held_ref[:, : 3 * width]) * gain
    widened = x_ref[:, :depth].astype(jnp.float32)
    centered = widened - jnp.mean(widened, axis=-1, keepdims=True)
    normal_form = centered * inverse
    branch = inverse * (
        scaled
        - jnp.mean(scaled, axis=-1, keepdims=True)
        - normal_form * jnp.mean(scaled * normal_form, axis=-1, keepdims=True)
    )
    out_ref[...] = branch.astype(out_ref.dtype)


def temporal(mixed, gain, pieces, places, width, patches):
    tokens, depth = mixed.shape[0], gain.shape[1]
    held = max(2 * pieces[0].shape[2], 3 * width) if len(pieces) > 1 else pieces[0].shape[2]
    count = sum(piece.shape[0] for piece in pieces)
    return pl.pallas_call(
        functools.partial(temporal_kernel, patches, len(pieces)),
        out_shape=jax.ShapeDtypeStruct((tokens, depth), jnp.bfloat16),
        in_specs=[pl.BlockSpec(memory_space=pltpu.SMEM)]
        + [pl.BlockSpec(memory_space=pltpu.VMEM)] * 2
        + [pl.BlockSpec(memory_space=pl.ANY)] * len(pieces),
        out_specs=pl.BlockSpec(memory_space=pltpu.VMEM),
        scratch_shapes=[
            pltpu.VMEM((tokens, tokens), jnp.float32),
            pltpu.VMEM((tokens, 3 * width), jnp.bfloat16),
            pltpu.VMEM((tokens, width), jnp.bfloat16),
            pltpu.VMEM((tokens, 3 * width), jnp.bfloat16),
            pltpu.VMEM((tokens, width), jnp.bfloat16),
            pltpu.VMEM((depth, held), jnp.bfloat16),
            pltpu.SemaphoreType.DMA((count,)),
        ],
        compiler_params=pltpu.CompilerParams(vmem_limit_bytes=VMEM_LIMIT),
        cost_estimate=pl.CostEstimate(
            flops=12 * tokens * depth * width + 12 * HEADS * tokens * tokens * 2 * LANES,
            bytes_accessed=2 * (2 * tokens * 3 * width + 3 * depth * width),
            transcendentals=HEADS * tokens * tokens,
        ),
        name="temporal_backward",
    )(places, mixed, gain, *pieces)


def prepare_kernel(count, place_ref, stream_ref, *refs):
    pieces, refs = refs[:count], refs[count:]
    weights_refs = refs[:PARTS]
    held_stream_ref, held_ref, sems = refs[PARTS:]
    copies = []
    for piece in pieces:
        for slot in range(piece.shape[0]):
            number = len(copies)
            if piece.shape[2] == held_ref.shape[2]:
                target = held_ref.at[slot]
            else:
                column = pl.multiple_of(place_ref[2 * number + 1], piece.shape[2])
                target = held_ref.at[place_ref[2 * number], :, pl.ds(column, piece.shape[2])]
            copies.append(pltpu.make_async_copy(piece.at[slot], target, sems.at[number]))
            copies[-1].start()
    held_stream_ref[...] = stream_ref[...]
    for copy in copies:
        copy.wait()
    blocks = [held_ref[chip].astype(jnp.float32) for chip in range(held_ref.shape[0])]
    joined = jnp.concatenate(blocks, axis=0)
    for index, part in enumerate(weights_refs):
        rows, depth = part.shape
        part[...] = joined[index * rows : (index + 1) * rows, :depth].astype(part.dtype)


def prepare(stream, pieces, places, width):
    tokens, depth = stream.shape
    rows = pieces[0].shape[1]
    held = max(depth, pieces[0].shape[2] * (1 if len(pieces) == 1 else 2))
    count = sum(piece.shape[0] for piece in pieces)
    return pl.pallas_call(
        functools.partial(prepare_kernel, len(pieces)),
        out_shape=(jax.ShapeDtypeStruct((width // PARTS, depth), jnp.bfloat16),) * PARTS
        + (jax.ShapeDtypeStruct((tokens, depth), jnp.bfloat16),),
        in_specs=[pl.BlockSpec(memory_space=pltpu.SMEM)]
        + [pl.BlockSpec(memory_space=pltpu.VMEM)]
        + [pl.BlockSpec(memory_space=pl.ANY)] * len(pieces),
        out_specs=(pl.BlockSpec(memory_space=pltpu.VMEM),) * (PARTS + 1),
        scratch_shapes=[
            pltpu.VMEM((width // rows, rows, held), jnp.bfloat16),
            pltpu.SemaphoreType.DMA((count,)),
        ],
        compiler_params=pltpu.CompilerParams(vmem_limit_bytes=VMEM_LIMIT),
        cost_estimate=pl.CostEstimate(
            flops=0, bytes_accessed=4 * depth * (tokens + width), transcendentals=0
        ),
        name="spatial_prepare",
    )(places, stream, *pieces)


def attention_of(saved_ref, head):
    scores_t = dot_tn(saved_ref[1, head], saved_ref[0, head])
    return soft(scores_t, 1.0 / math.sqrt(HD)).astype(jnp.bfloat16)


def spatial_kernel(saved_ref, stream_ref, branch_ref, *refs):
    w_refs, (hidden_ref, out_ref) = refs[:-2], refs[-2:]
    scale = 1.0 / math.sqrt(HD)
    hidden_grad = (
        stream_ref[...].astype(jnp.float32) + branch_ref[...].astype(jnp.float32)
    ).astype(jnp.bfloat16)
    hidden_ref[...] = hidden_grad
    grad_all = jnp.concatenate([dot_nt(w_ref[...], hidden_grad) for w_ref in w_refs], axis=0)
    for head in range(HEADS):
        grad_o = grad_all[head * HD : (head + 1) * HD].astype(jnp.bfloat16)
        rounded_t = attention_of(saved_ref, head)
        wide = rounded_t.astype(jnp.float32)
        spread_t = dot_tn(saved_ref[2, head], grad_o)
        delta = jnp.sum(wide * spread_t, axis=0, keepdims=True)
        dscore_t = (wide * (spread_t - delta)).astype(jnp.bfloat16)
        out_ref[0, head] = (dot_nn(saved_ref[1, head], dscore_t) * scale).astype(out_ref.dtype)
        out_ref[1, head] = (dot_nt(saved_ref[0, head], dscore_t) * scale).astype(out_ref.dtype)
        out_ref[2, head] = dot_nt(grad_o, rounded_t).astype(out_ref.dtype)


def spatial(saved, stream, branch, weights):
    tokens, depth = stream.shape
    width = HEADS * HD
    return pl.pallas_call(
        spatial_kernel,
        out_shape=(
            jax.ShapeDtypeStruct((tokens, depth), jnp.bfloat16),
            jax.ShapeDtypeStruct((3, HEADS, HD, tokens), jnp.bfloat16),
        ),
        compiler_params=pltpu.CompilerParams(vmem_limit_bytes=VMEM_LIMIT),
        cost_estimate=pl.CostEstimate(
            flops=2 * tokens * depth * width + 10 * HEADS * tokens * tokens * 2 * LANES,
            bytes_accessed=2 * (3 * tokens * depth + depth * width + 6 * tokens * width),
            transcendentals=HEADS * tokens * tokens,
        ),
        name="spatial_backward",
    )(saved, stream, branch, *weights)


def moved(block, clips, devices, target):
    pairs = []
    for clip in range(clips):
        for own in range(devices):
            x, y, z, core = target(clip, own // 2 % 2, own // 4, own % 2)
            pairs.append((clip * devices + own, x * devices + (2 * z + y) * 2 + core))
    return lax.ppermute(block, ("clip", "seq"), pairs)


def half_of(columns):
    return -(-columns // (2 * LANES)) * LANES


class Gather:
    def __init__(self, clips, devices):
        self.send = functools.partial(moved, clips=clips, devices=devices)
        clip, own = lax.axis_index("clip"), lax.axis_index("seq")
        self.x, self.core, self.y, self.z = clip % 2, own % 2, own // 2 % 2, own // 4
        self.pairs = devices // 8

    def block(self, weights):
        other = self.send(weights, target=lambda x, y, z, core: (x, y, z, 1 - core))
        rows = jnp.where(
            self.core == 0,
            jnp.concatenate([weights, other]),
            jnp.concatenate([other, weights]),
        )
        half = half_of(weights.shape[1])
        padded = jnp.pad(rows, ((0, 0), (0, 2 * half - weights.shape[1])))
        return jnp.where(self.x == 0, padded[:, :half], padded[:, half:])

    def along(self, block, late=None):
        return [
            self.send(
                block if pair or late is None else late,
                target=lambda x, y, z, core: (x, y, z ^ (2 * pair + core), core),
            )
            for pair in range(self.pairs)
        ]

    def beside(self, first):
        second = self.send(
            first,
            target=lambda x, y, z, core: (x, 1 - y, z, core) if core else (x ^ 1, y, z, core),
        )
        return first, second

    def across(self, both):
        rest = self.send(
            both,
            target=lambda x, y, z, core: (x ^ 1, y, z, core) if core else (x, 1 - y, z, core),
        )
        return jnp.concatenate([both, rest])

    def swap(self, four):
        return self.send(four, target=lambda x, y, z, core: (x, y, z, 1 - core))

    def places(self, pairs, rows, half):
        found = []
        for parity in (self.core, 1 - self.core):
            for slot in range(4):
                for pair in pairs:
                    far_x = jnp.where(parity == 0, slot % 2, slot // 2)
                    far_y = jnp.where(parity == 0, slot // 2, slot % 2)
                    chip = 2 * (self.z ^ (2 * pair + parity)) + (self.y ^ far_y)
                    found += [rows * chip, half * (self.x ^ far_x)]
        return found


def tied(first, second):
    return lax.optimization_barrier((first, second))


def shards(
    clips,
    spatial_saved,
    hidden,
    temporal_out_grad,
    stream_grad,
    modulation,
    temporal_weights,
    spatial_weights,
):
    frames = lax.axis_size("seq")
    tokens, depth = hidden.shape[1:]
    width = temporal_out_grad.shape[2]
    patches = tokens // frames
    chips = frames // 2
    gain = 1.0 + modulation.reshape(1, depth)
    saved = spatial_saved.transpose(0, 1, 3, 2).reshape(3, HEADS, HD, tokens)
    mixed = jnp.concatenate([hidden, temporal_out_grad], axis=2).reshape(frames, patches, depth + width)
    if clips % 2 == 0 and chips >= 4 and chips & (chips - 1) == 0 and 2 * depth // frames % 16 == 0:
        gather = Gather(clips, frames)
        block = gather.block(temporal_weights)
        late, mixed = tied(block, mixed)
        firsts = gather.along(block, late)
        rows, half = firsts[0].shape
        places = [place for pair in range(len(firsts)) for place in gather.places([pair], rows, half)]
        small_places = gather.places(range(len(firsts)), 1, half_of(depth))
        places, small_places = (jnp.stack(p).astype(jnp.int32) for p in (places, small_places))
        both = [jnp.concatenate(gather.beside(firsts[0][None]))]
        (both[0], firsts, spatial_weights, places, small_places, gain), mixed = tied(
            (both[0], firsts, spatial_weights, places, small_places, gain), mixed
        )
        mixed = lax.all_to_all(mixed, "seq", split_axis=0, concat_axis=0, tiled=True)
        both += [jnp.concatenate(gather.beside(first[None])) for first in firsts[1:]]
        small = jnp.stack(gather.along(gather.block(spatial_weights)))
        four = [gather.across(block) for block in both]
        (four[-1], small), mixed = tied((four[-1], small), mixed)
        pieces = [piece for block in four for piece in (block, gather.swap(block))]
        small = gather.beside(small)
    else:
        mixed = lax.all_to_all(mixed, "seq", split_axis=0, concat_axis=0, tiled=True)
        places = small_places = jnp.zeros((2,), jnp.int32)
        pieces = [lax.all_gather(temporal_weights, "seq", axis=0, tiled=True)[None]]
        gather, small_pieces = None, [lax.all_gather(spatial_weights, "seq", axis=0, tiled=True)[None]]
    branch = temporal(mixed.reshape(tokens, depth + width), gain, pieces, places, width, patches)
    if gather:
        small, branch = tied(small, branch)
        small = gather.across(jnp.concatenate(small))
        small_pieces = [small, gather.swap(small)]
    *parts, stream = prepare(
        stream_grad.reshape(tokens, depth), small_pieces, small_places, width
    )
    branch = lax.all_to_all(
        branch.reshape(frames, patches, depth), "seq", split_axis=0, concat_axis=0, tiled=True
    )
    hidden_grad, spatial_grad = spatial(
        saved, stream, branch.reshape(tokens, depth), parts
    )
    spatial_grad = spatial_grad.reshape(3, 1, width, tokens).transpose(0, 1, 3, 2)
    return (hidden_grad.reshape(1, tokens, depth), spatial_grad)


def solution(mesh):
    return jax.shard_map(
        functools.partial(shards, mesh.shape["clip"]),
        mesh=mesh,
        in_specs=(
            P(None, ("clip", "seq"), None, None),
            P(("clip", "seq"), None, None),
            P(("clip", "seq"), None, None),
            P(("clip", "seq"), None, None),
            P(),
            P("seq", None),
            P("seq", None),
        ),
        out_specs=(P(("clip", "seq"), None, None), P(None, ("clip", "seq"), None, None)),
        check_vma=False,
    )
```

```python
import functools
import math

import jax
import jax.numpy as jnp
from jax import lax
from jax.experimental import pallas as pl
from jax.experimental.pallas import tpu as pltpu
from jax.sharding import PartitionSpec as P

HEADS = 8
HD = 72
LANES = 128
PARTS = 3

epsilon = 1e-06
VMEM_LIMIT = 24 * 1024 * 1024


def window(head, width):
    low, high = head * HD, (head + 1) * HD
    start = low // LANES * LANES
    stop = min(-(-high // LANES) * LANES, width)
    return start, stop, low, high


def keep(block, start, low, high):
    lane = lax.broadcasted_iota(jnp.int32, block.shape, 1) + start
    return jnp.where((lane >= low) & (lane < high), block, jnp.zeros_like(block))


def dot_nt(a, b):
    return lax.dot_general(a, b, (((1,), (1,)), ((), ())), preferred_element_type=jnp.float32)


def dot_tn(a, b):
    return lax.dot_general(a, b, (((0,), (0,)), ((), ())), preferred_element_type=jnp.float32)


def dot_nn(a, b):
    return jnp.dot(a, b, preferred_element_type=jnp.float32)


def soft(scores_t, scale):
    top = jnp.max(scores_t, axis=0, keepdims=True)
    raised = jnp.exp2((scores_t - top) * (scale * math.log2(math.e)))
    return raised * (1.0 / jnp.sum(raised, axis=0, keepdims=True))


class Tiles:
    def __init__(self):
        self.sums = {}

    def add(self, start, part):
        for offset in range(0, part.shape[1], LANES):
            piece = part[:, offset : offset + LANES]
            key = start + offset
            self.sums[key] = self.sums[key] + piece if key in self.sums else piece

    def store(self, ref, base, width, scale, upto):
        for key in sorted(self.sums):
            stop = min(key + LANES, width)
            if stop <= upto:
                done = self.sums.pop(key)[:, : stop - key] * scale
                ref[:, base + key : base + stop] = done.astype(ref.dtype)


def head_grads(attention_t, query, keys, values, grad_o, start, low, high):
    rounded_t = attention_t.astype(jnp.bfloat16)
    spread_t = dot_nt(keep(values, start, low, high), grad_o)
    wide = rounded_t.astype(jnp.float32)
    delta = jnp.sum(wide * spread_t, axis=0, keepdims=True)
    dscore_t = (attention_t.astype(jnp.float32) * (spread_t - delta)).astype(jnp.bfloat16)
    return (
        dot_tn(dscore_t, keep(keys, start, low, high)),
        dot_nn(dscore_t, keep(query, start, low, high)),
        dot_nn(rounded_t, keep(grad_o, start, low, high)),
    )


def temporal_kernel(patches, count, place_ref, x_ref, gain_ref, *refs):
    pieces, refs = refs[:count], refs[count:]
    out_ref, bias_ref, proj_ref, keys_ref, grad_ref, gk_ref, held_ref, sems = refs
    tokens, depth = out_ref.shape
    width = keys_ref.shape[1]
    scale = 1.0 / math.sqrt(HD)
    copies = []
    for index, piece in enumerate(pieces):
        for slot in range(piece.shape[0]):
            rows, columns = piece.shape[1:]
            number = len(copies)
            if rows == depth:
                copies.append(pltpu.make_async_copy(piece.at[slot], held_ref, sems.at[number]))
                copies[-1].start()
                continue
            row = pl.multiple_of(place_ref[2 * number], rows)
            column = pl.multiple_of(place_ref[2 * number + 1], columns)
            copies.append(
                pltpu.make_async_copy(
                    piece.at[slot],
                    held_ref.at[pl.ds(row, rows), pl.ds(column, columns)],
                    sems.at[number],
                )
            )
            copies[-1].start()
    row = lax.broadcasted_iota(jnp.int32, (tokens, tokens), 0)
    column = lax.broadcasted_iota(jnp.int32, (tokens, tokens), 1)
    bias_ref[...] = jnp.where(lax.rem(row, patches) == lax.rem(column, patches), 0.0, -1e30)
    gain = gain_ref[...]
    widened = x_ref[:, :depth].astype(jnp.float32)
    centered = widened - jnp.mean(widened, axis=-1, keepdims=True)
    inverse = lax.rsqrt(jnp.mean(centered * centered, axis=-1, keepdims=True) + epsilon)
    normed = (centered * inverse * gain).astype(jnp.bfloat16)
    for copy in copies:
        copy.wait()
    proj_ref[...] = dot_nn(normed, held_ref[:, : 3 * width]).astype(jnp.bfloat16)
    keys_ref[...] = proj_ref[:, width : 2 * width]
    sums = [Tiles(), Tiles(), Tiles()]
    for head in range(HEADS):
        start, stop, low, high = window(head, width)
        query = proj_ref[:, start:stop]
        keys = keys_ref[:, start:stop]
        values = proj_ref[:, 2 * width + start : 2 * width + stop]
        grad_o = x_ref[:, depth + start : depth + stop]
        scores_t = dot_nt(keep(keys, start, low, high), query) + bias_ref[...]
        parts = head_grads(soft(scores_t, scale), query, keys, values, grad_o, start, low, high)
        for tiles, part in zip(sums, parts):
            tiles.add(start, part)
        upto = width if head == HEADS - 1 else high // LANES * LANES
        sums[0].store(grad_ref, 0, width, scale, upto)
        sums[1].store(gk_ref, 0, width, scale, upto)
        sums[2].store(grad_ref, 2 * width, width, 1.0, upto)
    grad_ref[:, width : 2 * width] = gk_ref[...]
    scaled = dot_nt(grad_ref[...], held_ref[:, : 3 * width]) * gain
    widened = x_ref[:, :depth].astype(jnp.float32)
    centered = widened - jnp.mean(widened, axis=-1, keepdims=True)
    normal_form = centered * inverse
    branch = inverse * (
        scaled
        - jnp.mean(scaled, axis=-1, keepdims=True)
        - normal_form * jnp.mean(scaled * normal_form, axis=-1, keepdims=True)
    )
    out_ref[...] = branch.astype(out_ref.dtype)


def temporal(mixed, gain, pieces, places, width, patches):
    tokens, depth = mixed.shape[0], gain.shape[1]
    held = max(2 * pieces[0].shape[2], 3 * width) if len(pieces) > 1 else pieces[0].shape[2]
    count = sum(piece.shape[0] for piece in pieces)
    return pl.pallas_call(
        functools.partial(temporal_kernel, patches, len(pieces)),
        out_shape=jax.ShapeDtypeStruct((tokens, depth), jnp.bfloat16),
        in_specs=[pl.BlockSpec(memory_space=pltpu.SMEM)]
        + [pl.BlockSpec(memory_space=pltpu.VMEM)] * 2
        + [pl.BlockSpec(memory_space=pl.ANY)] * len(pieces),
        out_specs=pl.BlockSpec(memory_space=pltpu.VMEM),
        scratch_shapes=[
            pltpu.VMEM((tokens, tokens), jnp.float32),
            pltpu.VMEM((tokens, 3 * width), jnp.bfloat16),
            pltpu.VMEM((tokens, width), jnp.bfloat16),
            pltpu.VMEM((tokens, 3 * width), jnp.bfloat16),
            pltpu.VMEM((tokens, width), jnp.bfloat16),
            pltpu.VMEM((depth, held), jnp.bfloat16),
            pltpu.SemaphoreType.DMA((count,)),
        ],
        compiler_params=pltpu.CompilerParams(vmem_limit_bytes=VMEM_LIMIT),
        cost_estimate=pl.CostEstimate(
            flops=12 * tokens * depth * width + 12 * HEADS * tokens * tokens * 2 * LANES,
            bytes_accessed=2 * (2 * tokens * 3 * width + 3 * depth * width),
            transcendentals=HEADS * tokens * tokens,
        ),
        name="temporal_backward",
    )(places, mixed, gain, *pieces)


def prepare_kernel(count, place_ref, stream_ref, *refs):
    pieces, refs = refs[:count], refs[count:]
    weights_refs = refs[:PARTS]
    held_stream_ref, held_ref, sems = refs[PARTS:]
    copies = []
    for piece in pieces:
        for slot in range(piece.shape[0]):
            number = len(copies)
            if piece.shape[2] == held_ref.shape[2]:
                target = held_ref.at[slot]
            else:
                column = pl.multiple_of(place_ref[2 * number + 1], piece.shape[2])
                target = held_ref.at[place_ref[2 * number], :, pl.ds(column, piece.shape[2])]
            copies.append(pltpu.make_async_copy(piece.at[slot], target, sems.at[number]))
            copies[-1].start()
    held_stream_ref[...] = stream_ref[...]
    for copy in copies:
        copy.wait()
    blocks = [held_ref[chip].astype(jnp.float32) for chip in range(held_ref.shape[0])]
    joined = jnp.concatenate(blocks, axis=0)
    for index, part in enumerate(weights_refs):
        rows, depth = part.shape
        part[...] = joined[index * rows : (index + 1) * rows, :depth].astype(part.dtype)


def prepare(stream, pieces, places, width):
    tokens, depth = stream.shape
    rows = pieces[0].shape[1]
    held = max(depth, pieces[0].shape[2] * (1 if len(pieces) == 1 else 2))
    count = sum(piece.shape[0] for piece in pieces)
    return pl.pallas_call(
        functools.partial(prepare_kernel, len(pieces)),
        out_shape=(jax.ShapeDtypeStruct((width // PARTS, depth), jnp.bfloat16),) * PARTS
        + (jax.ShapeDtypeStruct((tokens, depth), jnp.bfloat16),),
        in_specs=[pl.BlockSpec(memory_space=pltpu.SMEM)]
        + [pl.BlockSpec(memory_space=pltpu.VMEM)]
        + [pl.BlockSpec(memory_space=pl.ANY)] * len(pieces),
        out_specs=(pl.BlockSpec(memory_space=pltpu.VMEM),) * (PARTS + 1),
        scratch_shapes=[
            pltpu.VMEM((width // rows, rows, held), jnp.bfloat16),
            pltpu.SemaphoreType.DMA((count,)),
        ],
        compiler_params=pltpu.CompilerParams(vmem_limit_bytes=VMEM_LIMIT),
        cost_estimate=pl.CostEstimate(
            flops=0, bytes_accessed=4 * depth * (tokens + width), transcendentals=0
        ),
        name="spatial_prepare",
    )(places, stream, *pieces)


def attention_of(saved_ref, head):
    scores_t = dot_tn(saved_ref[1, head], saved_ref[0, head])
    return soft(scores_t, 1.0 / math.sqrt(HD)).astype(jnp.bfloat16)


def spatial_kernel(saved_ref, stream_ref, branch_ref, *refs):
    w_refs, (hidden_ref, out_ref) = refs[:-2], refs[-2:]
    scale = 1.0 / math.sqrt(HD)
    hidden_grad = (
        stream_ref[...].astype(jnp.float32) + branch_ref[...].astype(jnp.float32)
    ).astype(jnp.bfloat16)
    hidden_ref[...] = hidden_grad
    grad_all = jnp.concatenate([dot_nt(w_ref[...], hidden_grad) for w_ref in w_refs], axis=0)
    for head in range(HEADS):
        grad_o = grad_all[head * HD : (head + 1) * HD].astype(jnp.bfloat16)
        rounded_t = attention_of(saved_ref, head)
        wide = rounded_t.astype(jnp.float32)
        spread_t = dot_tn(saved_ref[2, head], grad_o)
        delta = jnp.sum(wide * spread_t, axis=0, keepdims=True)
        dscore_t = (wide * (spread_t - delta)).astype(jnp.bfloat16)
        out_ref[0, head] = (dot_nn(saved_ref[1, head], dscore_t) * scale).astype(out_ref.dtype)
        out_ref[1, head] = (dot_nt(saved_ref[0, head], dscore_t) * scale).astype(out_ref.dtype)
        out_ref[2, head] = dot_nt(grad_o, rounded_t).astype(out_ref.dtype)


def spatial(saved, stream, branch, weights):
    tokens, depth = stream.shape
    width = HEADS * HD
    return pl.pallas_call(
        spatial_kernel,
        out_shape=(
            jax.ShapeDtypeStruct((tokens, depth), jnp.bfloat16),
            jax.ShapeDtypeStruct((3, HEADS, HD, tokens), jnp.bfloat16),
        ),
        compiler_params=pltpu.CompilerParams(vmem_limit_bytes=VMEM_LIMIT),
        cost_estimate=pl.CostEstimate(
            flops=2 * tokens * depth * width + 10 * HEADS * tokens * tokens * 2 * LANES,
            bytes_accessed=2 * (3 * tokens * depth + depth * width + 6 * tokens * width),
            transcendentals=HEADS * tokens * tokens,
        ),
        name="spatial_backward",
    )(saved, stream, branch, *weights)


def moved(block, clips, devices, target):
    pairs = []
    for clip in range(clips):
        for own in range(devices):
            x, y, z, core = target(clip, own // 2 % 2, own // 4, own % 2)
            pairs.append((clip * devices + own, x * devices + (2 * z + y) * 2 + core))
    return lax.ppermute(block, ("clip", "seq"), pairs)


def half_of(columns):
    return -(-columns // (2 * LANES)) * LANES


class Gather:
    def __init__(self, clips, devices):
        self.send = functools.partial(moved, clips=clips, devices=devices)
        clip, own = lax.axis_index("clip"), lax.axis_index("seq")
        self.x, self.core, self.y, self.z = clip % 2, own % 2, own // 2 % 2, own // 4
        self.pairs = devices // 8

    def block(self, weights):
        other = self.send(weights, target=lambda x, y, z, core: (x, y, z, 1 - core))
        rows = jnp.where(
            self.core == 0,
            jnp.concatenate([weights, other]),
            jnp.concatenate([other, weights]),
        )
        half = half_of(weights.shape[1])
        padded = jnp.pad(rows, ((0, 0), (0, 2 * half - weights.shape[1])))
        return jnp.where(self.x == 0, padded[:, :half], padded[:, half:])

    def along(self, block, late=None):
        return [
            self.send(
                block if pair or late is None else late,
                target=lambda x, y, z, core: (x, y, z ^ (2 * pair + core), core),
            )
            for pair in range(self.pairs)
        ]

    def beside(self, first):
        second = self.send(
            first,
            target=lambda x, y, z, core: (x, 1 - y, z, core) if core else (x ^ 1, y, z, core),
        )
        return first, second

    def across(self, both):
        rest = self.send(
            both,
            target=lambda x, y, z, core: (x ^ 1, y, z, core) if core else (x, 1 - y, z, core),
        )
        return jnp.concatenate([both, rest])

    def swap(self, four):
        return self.send(four, target=lambda x, y, z, core: (x, y, z, 1 - core))

    def places(self, pairs, rows, half):
        found = []
        for parity in (self.core, 1 - self.core):
            for slot in range(4):
                for pair in pairs:
                    far_x = jnp.where(parity == 0, slot % 2, slot // 2)
                    far_y = jnp.where(parity == 0, slot // 2, slot % 2)
                    chip = 2 * (self.z ^ (2 * pair + parity)) + (self.y ^ far_y)
                    found += [rows * chip, half * (self.x ^ far_x)]
        return found


def tied(first, second):
    return lax.optimization_barrier((first, second))


def shards(
    clips,
    spatial_saved,
    hidden,
    temporal_out_grad,
    stream_grad,
    modulation,
    temporal_weights,
    spatial_weights,
):
    frames = lax.axis_size("seq")
    tokens, depth = hidden.shape[1:]
    width = temporal_out_grad.shape[2]
    patches = tokens // frames
    chips = frames // 2
    gain = 1.0 + modulation.reshape(1, depth)
    saved = spatial_saved.transpose(0, 1, 3, 2).reshape(3, HEADS, HD, tokens)
    mixed = jnp.concatenate([hidden, temporal_out_grad], axis=2).reshape(frames, patches, depth + width)
    if clips % 2 == 0 and chips >= 4 and chips & (chips - 1) == 0 and 2 * depth // frames % 16 == 0:
        gather = Gather(clips, frames)
        block = gather.block(temporal_weights)
        late, mixed = tied(block, mixed)
        firsts = gather.along(block, late)
        rows, half = firsts[0].shape
        places = [place for pair in range(len(firsts)) for place in gather.places([pair], rows, half)]
        small_places = gather.places(range(len(firsts)), 1, half_of(depth))
        places, small_places = (jnp.stack(p).astype(jnp.int32) for p in (places, small_places))
        both = [jnp.concatenate(gather.beside(firsts[0][None]))]
        (both[0], firsts, spatial_weights, places, small_places, gain), mixed = tied(
            (both[0], firsts, spatial_weights, places, small_places, gain), mixed
        )
        mixed = lax.all_to_all(mixed, "seq", split_axis=0, concat_axis=0, tiled=True)
        both += [jnp.concatenate(gather.beside(first[None])) for first in firsts[1:]]
        small = jnp.stack(gather.along(gather.block(spatial_weights)))
        four = [gather.across(block) for block in both]
        (four[-1], small), mixed = tied((four[-1], small), mixed)
        pieces = [piece for block in four for piece in (block, gather.swap(block))]
        small = gather.beside(small)
    else:
        mixed = lax.all_to_all(mixed, "seq", split_axis=0, concat_axis=0, tiled=True)
        places = small_places = jnp.zeros((2,), jnp.int32)
        pieces = [lax.all_gather(temporal_weights, "seq", axis=0, tiled=True)[None]]
        gather, small_pieces = None, [lax.all_gather(spatial_weights, "seq", axis=0, tiled=True)[None]]
    branch = temporal(mixed.reshape(tokens, depth + width), gain, pieces, places, width, patches)
    if gather:
        small, branch = tied(small, branch)
        small = gather.across(jnp.concatenate(small))
        small_pieces = [small, gather.swap(small)]
    *parts, stream = prepare(
        stream_grad.reshape(tokens, depth), small_pieces, small_places, width
    )
    branch = lax.all_to_all(
        branch.reshape(frames, patches, depth), "seq", split_axis=0, concat_axis=0, tiled=True
    )
    hidden_grad, spatial_grad = spatial(
        saved, stream, branch.reshape(tokens, depth), parts
    )
    spatial_grad = spatial_grad.reshape(3, 1, width, tokens).transpose(0, 1, 3, 2)
    return (hidden_grad.reshape(1, tokens, depth), spatial_grad)


def solution(mesh):
    return jax.shard_map(
        functools.partial(shards, mesh.shape["clip"]),
        mesh=mesh,
        in_specs=(
            P(None, ("clip", "seq"), None, None),
            P(("clip", "seq"), None, None),
            P(("clip", "seq"), None, None),
            P(("clip", "seq"), None, None),
            P(),
            P("seq", None),
            P("seq", None),
        ),
        out_specs=(P(("clip", "seq"), None, None), P(None, ("clip", "seq"), None, None)),
        check_vma=False,
    )
```

```python
import functools
import math

import jax
import jax.numpy as jnp
from jax import lax
from jax.experimental import pallas as pl
from jax.experimental.pallas import tpu as pltpu
from jax.sharding import PartitionSpec as P

HEADS = 8
HD = 72
LANES = 128
PARTS = 3

epsilon = 1e-06
VMEM_LIMIT = 24 * 1024 * 1024


def window(head, width):
    low, high = head * HD, (head + 1) * HD
    start = low // LANES * LANES
    stop = min(-(-high // LANES) * LANES, width)
    return start, stop, low, high


def keep(block, start, low, high):
    lane = lax.broadcasted_iota(jnp.int32, block.shape, 1) + start
    return jnp.where((lane >= low) & (lane < high), block, jnp.zeros_like(block))


def dot_nt(a, b):
    return lax.dot_general(a, b, (((1,), (1,)), ((), ())), preferred_element_type=jnp.float32)


def dot_tn(a, b):
    return lax.dot_general(a, b, (((0,), (0,)), ((), ())), preferred_element_type=jnp.float32)


def dot_nn(a, b):
    return jnp.dot(a, b, preferred_element_type=jnp.float32)


def soft(scores_t, scale):
    top = jnp.max(scores_t, axis=0, keepdims=True)
    raised = jnp.exp2((scores_t - top) * (scale * math.log2(math.e)))
    return raised * (1.0 / jnp.sum(raised, axis=0, keepdims=True))


class Tiles:
    def __init__(self):
        self.sums = {}

    def add(self, start, part):
        for offset in range(0, part.shape[1], LANES):
            piece = part[:, offset : offset + LANES]
            key = start + offset
            self.sums[key] = self.sums[key] + piece if key in self.sums else piece

    def store(self, ref, base, width, scale, upto):
        for key in sorted(self.sums):
            stop = min(key + LANES, width)
            if stop <= upto:
                done = self.sums.pop(key)[:, : stop - key] * scale
                ref[:, base + key : base + stop] = done.astype(ref.dtype)


def head_grads(attention_t, query, keys, values, grad_o, start, low, high):
    rounded_t = attention_t.astype(jnp.bfloat16)
    spread_t = dot_nt(keep(values, start, low, high), grad_o)
    wide = rounded_t.astype(jnp.float32)
    delta = jnp.sum(wide * spread_t, axis=0, keepdims=True)
    dscore_t = (wide * (spread_t - delta)).astype(jnp.bfloat16)
    return (
        dot_tn(dscore_t, keep(keys, start, low, high)),
        dot_nn(dscore_t, keep(query, start, low, high)),
        dot_nn(rounded_t, keep(grad_o, start, low, high)),
    )


def temporal_kernel(patches, count, place_ref, x_ref, gain_ref, *refs):
    pieces, refs = refs[:count], refs[count:]
    out_ref, bias_ref, proj_ref, keys_ref, grad_ref, gk_ref, held_ref, sems = refs
    tokens, depth = out_ref.shape
    width = keys_ref.shape[1]
    scale = 1.0 / math.sqrt(HD)
    copies = []
    for index, piece in enumerate(pieces):
        for slot in range(piece.shape[0]):
            rows, columns = piece.shape[1:]
            number = len(copies)
            if rows == depth:
                copies.append(pltpu.make_async_copy(piece.at[slot], held_ref, sems.at[number]))
                copies[-1].start()
                continue
            row = pl.multiple_of(place_ref[2 * number], rows)
            column = pl.multiple_of(place_ref[2 * number + 1], columns)
            copies.append(
                pltpu.make_async_copy(
                    piece.at[slot],
                    held_ref.at[pl.ds(row, rows), pl.ds(column, columns)],
                    sems.at[number],
                )
            )
            copies[-1].start()
    row = lax.broadcasted_iota(jnp.int32, (tokens, tokens), 0)
    column = lax.broadcasted_iota(jnp.int32, (tokens, tokens), 1)
    bias_ref[...] = jnp.where(lax.rem(row, patches) == lax.rem(column, patches), 0.0, -1e30)
    gain = gain_ref[...]
    widened = x_ref[:, :depth].astype(jnp.float32)
    mean = jnp.mean(widened, axis=-1, keepdims=True)
    centered = widened - mean
    inverse = lax.rsqrt(jnp.mean(centered * centered, axis=-1, keepdims=True) + epsilon)
    normed = (centered * inverse * gain).astype(jnp.bfloat16)
    for copy in copies:
        copy.wait()
    proj_ref[...] = dot_nn(normed, held_ref[:, : 3 * width]).astype(jnp.bfloat16)
    keys_ref[...] = proj_ref[:, width : 2 * width]
    sums = [Tiles(), Tiles(), Tiles()]
    for head in range(HEADS):
        start, stop, low, high = window(head, width)
        query = proj_ref[:, start:stop]
        keys = keys_ref[:, start:stop]
        values = proj_ref[:, 2 * width + start : 2 * width + stop]
        grad_o = x_ref[:, depth + start : depth + stop]
        scores_t = dot_nt(keep(keys, start, low, high), query) + bias_ref[...]
        parts = head_grads(soft(scores_t, scale), query, keys, values, grad_o, start, low, high)
        for tiles, part in zip(sums, parts):
            tiles.add(start, part)
        upto = width if head == HEADS - 1 else high // LANES * LANES
        sums[0].store(grad_ref, 0, width, scale, upto)
        sums[1].store(gk_ref, 0, width, scale, upto)
        sums[2].store(grad_ref, 2 * width, width, 1.0, upto)
    grad_ref[:, width : 2 * width] = gk_ref[...]
    scaled = dot_nt(grad_ref[...], held_ref[:, : 3 * width]) * gain
    widened = x_ref[:, :depth].astype(jnp.float32)
    centered = widened - mean
    normal_form = centered * inverse
    branch = inverse * (
        scaled
        - jnp.mean(scaled, axis=-1, keepdims=True)
        - normal_form * jnp.mean(scaled * normal_form, axis=-1, keepdims=True)
    )
    out_ref[...] = branch.astype(out_ref.dtype)


def temporal(mixed, gain, pieces, places, width, patches):
    tokens, depth = mixed.shape[0], gain.shape[1]
    held = max(2 * pieces[0].shape[2], 3 * width) if len(pieces) > 1 else pieces[0].shape[2]
    count = sum(piece.shape[0] for piece in pieces)
    return pl.pallas_call(
        functools.partial(temporal_kernel, patches, len(pieces)),
        out_shape=jax.ShapeDtypeStruct((tokens, depth), jnp.bfloat16),
        in_specs=[pl.BlockSpec(memory_space=pltpu.SMEM)]
        + [pl.BlockSpec(memory_space=pltpu.VMEM)] * 2
        + [pl.BlockSpec(memory_space=pl.ANY)] * len(pieces),
        out_specs=pl.BlockSpec(memory_space=pltpu.VMEM),
        scratch_shapes=[
            pltpu.VMEM((tokens, tokens), jnp.float32),
            pltpu.VMEM((tokens, 3 * width), jnp.bfloat16),
            pltpu.VMEM((tokens, width), jnp.bfloat16),
            pltpu.VMEM((tokens, 3 * width), jnp.bfloat16),
            pltpu.VMEM((tokens, width), jnp.bfloat16),
            pltpu.VMEM((depth, held), jnp.bfloat16),
            pltpu.SemaphoreType.DMA((count,)),
        ],
        compiler_params=pltpu.CompilerParams(vmem_limit_bytes=VMEM_LIMIT),
        cost_estimate=pl.CostEstimate(
            flops=12 * tokens * depth * width + 12 * HEADS * tokens * tokens * 2 * LANES,
            bytes_accessed=2 * (2 * tokens * 3 * width + 3 * depth * width),
            transcendentals=HEADS * tokens * tokens,
        ),
        name="temporal_backward",
    )(places, mixed, gain, *pieces)


def prepare_kernel(count, place_ref, stream_ref, *refs):
    pieces, refs = refs[:count], refs[count:]
    weights_refs = refs[:PARTS]
    held_stream_ref, held_ref, sems = refs[PARTS:]
    copies = []
    for piece in pieces:
        for slot in range(piece.shape[0]):
            number = len(copies)
            if piece.shape[2] == held_ref.shape[2]:
                target = held_ref.at[slot]
            else:
                column = pl.multiple_of(place_ref[2 * number + 1], piece.shape[2])
                target = held_ref.at[place_ref[2 * number], :, pl.ds(column, piece.shape[2])]
            copies.append(pltpu.make_async_copy(piece.at[slot], target, sems.at[number]))
            copies[-1].start()
    held_stream_ref[...] = stream_ref[...]
    for copy in copies:
        copy.wait()
    blocks = [held_ref[chip].astype(jnp.float32) for chip in range(held_ref.shape[0])]
    joined = jnp.concatenate(blocks, axis=0)
    for index, part in enumerate(weights_refs):
        rows, depth = part.shape
        part[...] = joined[index * rows : (index + 1) * rows, :depth].astype(part.dtype)


def prepare(stream, pieces, places, width):
    tokens, depth = stream.shape
    rows = pieces[0].shape[1]
    held = max(depth, pieces[0].shape[2] * (1 if len(pieces) == 1 else 2))
    count = sum(piece.shape[0] for piece in pieces)
    return pl.pallas_call(
        functools.partial(prepare_kernel, len(pieces)),
        out_shape=(jax.ShapeDtypeStruct((width // PARTS, depth), jnp.bfloat16),) * PARTS
        + (jax.ShapeDtypeStruct((tokens, depth), jnp.bfloat16),),
        in_specs=[pl.BlockSpec(memory_space=pltpu.SMEM)]
        + [pl.BlockSpec(memory_space=pltpu.VMEM)]
        + [pl.BlockSpec(memory_space=pl.ANY)] * len(pieces),
        out_specs=(pl.BlockSpec(memory_space=pltpu.VMEM),) * (PARTS + 1),
        scratch_shapes=[
            pltpu.VMEM((width // rows, rows, held), jnp.bfloat16),
            pltpu.SemaphoreType.DMA((count,)),
        ],
        compiler_params=pltpu.CompilerParams(vmem_limit_bytes=VMEM_LIMIT),
        cost_estimate=pl.CostEstimate(
            flops=0, bytes_accessed=4 * depth * (tokens + width), transcendentals=0
        ),
        name="spatial_prepare",
    )(places, stream, *pieces)


def attention_of(saved_ref, head):
    scores_t = dot_tn(saved_ref[1, head], saved_ref[0, head])
    return soft(scores_t, 1.0 / math.sqrt(HD)).astype(jnp.bfloat16)


def spatial_kernel(saved_ref, stream_ref, branch_ref, *refs):
    w_refs, (hidden_ref, out_ref) = refs[:-2], refs[-2:]
    scale = 1.0 / math.sqrt(HD)
    hidden_grad = (
        stream_ref[...].astype(jnp.float32) + branch_ref[...].astype(jnp.float32)
    ).astype(jnp.bfloat16)
    hidden_ref[...] = hidden_grad
    grad_all = jnp.concatenate([dot_nt(w_ref[...], hidden_grad) for w_ref in w_refs], axis=0)
    for head in range(HEADS):
        grad_o = grad_all[head * HD : (head + 1) * HD].astype(jnp.bfloat16)
        rounded_t = attention_of(saved_ref, head)
        wide = rounded_t.astype(jnp.float32)
        spread_t = dot_tn(saved_ref[2, head], grad_o)
        delta = jnp.sum(wide * spread_t, axis=0, keepdims=True)
        dscore_t = (wide * (spread_t - delta)).astype(jnp.bfloat16)
        out_ref[0, head] = (dot_nn(saved_ref[1, head], dscore_t) * scale).astype(out_ref.dtype)
        out_ref[1, head] = (dot_nt(saved_ref[0, head], dscore_t) * scale).astype(out_ref.dtype)
        out_ref[2, head] = dot_nt(grad_o, rounded_t).astype(out_ref.dtype)


def spatial(saved, stream, branch, weights):
    tokens, depth = stream.shape
    width = HEADS * HD
    return pl.pallas_call(
        spatial_kernel,
        out_shape=(
            jax.ShapeDtypeStruct((tokens, depth), jnp.bfloat16),
            jax.ShapeDtypeStruct((3, HEADS, HD, tokens), jnp.bfloat16),
        ),
        compiler_params=pltpu.CompilerParams(vmem_limit_bytes=VMEM_LIMIT),
        cost_estimate=pl.CostEstimate(
            flops=2 * tokens * depth * width + 10 * HEADS * tokens * tokens * 2 * LANES,
            bytes_accessed=2 * (3 * tokens * depth + depth * width + 6 * tokens * width),
            transcendentals=HEADS * tokens * tokens,
        ),
        name="spatial_backward",
    )(saved, stream, branch, *weights)


def moved(block, clips, devices, target):
    pairs = []
    for clip in range(clips):
        for own in range(devices):
            x, y, z, core = target(clip, own // 2 % 2, own // 4, own % 2)
            pairs.append((clip * devices + own, x * devices + (2 * z + y) * 2 + core))
    return lax.ppermute(block, ("clip", "seq"), pairs)


def half_of(columns):
    return -(-columns // (2 * LANES)) * LANES


class Gather:
    def __init__(self, clips, devices):
        self.send = functools.partial(moved, clips=clips, devices=devices)
        clip, own = lax.axis_index("clip"), lax.axis_index("seq")
        self.x, self.core, self.y, self.z = clip % 2, own % 2, own // 2 % 2, own // 4
        self.pairs = devices // 8

    def block(self, weights):
        other = self.send(weights, target=lambda x, y, z, core: (x, y, z, 1 - core))
        rows = jnp.where(
            self.core == 0,
            jnp.concatenate([weights, other]),
            jnp.concatenate([other, weights]),
        )
        half = half_of(weights.shape[1])
        padded = jnp.pad(rows, ((0, 0), (0, 2 * half - weights.shape[1])))
        return jnp.where(self.x == 0, padded[:, :half], padded[:, half:])

    def along(self, block, late=None):
        return [
            self.send(
                block if pair or late is None else late,
                target=lambda x, y, z, core: (x, y, z ^ (2 * pair + core), core),
            )
            for pair in range(self.pairs)
        ]

    def beside(self, first):
        second = self.send(
            first,
            target=lambda x, y, z, core: (x, 1 - y, z, core) if core else (x ^ 1, y, z, core),
        )
        return first, second

    def across(self, both):
        rest = self.send(
            both,
            target=lambda x, y, z, core: (x ^ 1, y, z, core) if core else (x, 1 - y, z, core),
        )
        return jnp.concatenate([both, rest])

    def swap(self, four):
        return self.send(four, target=lambda x, y, z, core: (x, y, z, 1 - core))

    def places(self, pairs, rows, half):
        found = []
        for parity in (self.core, 1 - self.core):
            for slot in range(4):
                for pair in pairs:
                    far_x = jnp.where(parity == 0, slot % 2, slot // 2)
                    far_y = jnp.where(parity == 0, slot // 2, slot % 2)
                    chip = 2 * (self.z ^ (2 * pair + parity)) + (self.y ^ far_y)
                    found += [rows * chip, half * (self.x ^ far_x)]
        return found


def tied(first, second):
    return lax.optimization_barrier((first, second))


def shards(
    clips,
    spatial_saved,
    hidden,
    temporal_out_grad,
    stream_grad,
    modulation,
    temporal_weights,
    spatial_weights,
):
    frames = lax.axis_size("seq")
    tokens, depth = hidden.shape[1:]
    width = temporal_out_grad.shape[2]
    patches = tokens // frames
    chips = frames // 2
    gain = 1.0 + modulation.reshape(1, depth)
    saved = spatial_saved.transpose(0, 1, 3, 2).reshape(3, HEADS, HD, tokens)
    mixed = jnp.concatenate([hidden, temporal_out_grad], axis=2).reshape(frames, patches, depth + width)
    if clips % 2 == 0 and chips >= 4 and chips & (chips - 1) == 0 and 2 * depth // frames % 16 == 0:
        gather = Gather(clips, frames)
        block = gather.block(temporal_weights)
        late, mixed = tied(block, mixed)
        firsts = gather.along(block, late)
        rows, half = firsts[0].shape
        places = [place for pair in range(len(firsts)) for place in gather.places([pair], rows, half)]
        small_places = gather.places(range(len(firsts)), 1, half_of(depth))
        places, small_places = (jnp.stack(p).astype(jnp.int32) for p in (places, small_places))
        both = [jnp.concatenate(gather.beside(firsts[0][None]))]
        (both[0], firsts, spatial_weights, places, small_places, gain), mixed = tied(
            (both[0], firsts, spatial_weights, places, small_places, gain), mixed
        )
        mixed = lax.all_to_all(mixed, "seq", split_axis=0, concat_axis=0, tiled=True)
        both += [jnp.concatenate(gather.beside(first[None])) for first in firsts[1:]]
        small = jnp.stack(gather.along(gather.block(spatial_weights)))
        four = [gather.across(block) for block in both]
        (four[-1], small), mixed = tied((four[-1], small), mixed)
        pieces = [piece for block in four for piece in (block, gather.swap(block))]
        small = gather.beside(small)
    else:
        mixed = lax.all_to_all(mixed, "seq", split_axis=0, concat_axis=0, tiled=True)
        places = small_places = jnp.zeros((2,), jnp.int32)
        pieces = [lax.all_gather(temporal_weights, "seq", axis=0, tiled=True)[None]]
        gather, small_pieces = None, [lax.all_gather(spatial_weights, "seq", axis=0, tiled=True)[None]]
    branch = temporal(mixed.reshape(tokens, depth + width), gain, pieces, places, width, patches)
    if gather:
        small, branch = tied(small, branch)
        small = gather.across(jnp.concatenate(small))
        small_pieces = [small, gather.swap(small)]
    *parts, stream = prepare(
        stream_grad.reshape(tokens, depth), small_pieces, small_places, width
    )
    branch = lax.all_to_all(
        branch.reshape(frames, patches, depth), "seq", split_axis=0, concat_axis=0, tiled=True
    )
    hidden_grad, spatial_grad = spatial(
        saved, stream, branch.reshape(tokens, depth), parts
    )
    spatial_grad = spatial_grad.reshape(3, 1, width, tokens).transpose(0, 1, 3, 2)
    return (hidden_grad.reshape(1, tokens, depth), spatial_grad)


def solution(mesh):
    return jax.shard_map(
        functools.partial(shards, mesh.shape["clip"]),
        mesh=mesh,
        in_specs=(
            P(None, ("clip", "seq"), None, None),
            P(("clip", "seq"), None, None),
            P(("clip", "seq"), None, None),
            P(("clip", "seq"), None, None),
            P(),
            P("seq", None),
            P("seq", None),
        ),
        out_specs=(P(("clip", "seq"), None, None), P(None, ("clip", "seq"), None, None)),
        check_vma=False,
    )
```
